32 devices in a mesh: groups: 2 (over y), tiles: 4 (over z), band: 2 (over x), stokes: 2 (over core).
Axes of the slice: x: 2, y: 2, z: 4, core: 2. Of those that a mesh axis runs over, the one named last changes fastest.
Arguments:
- right_side: float32 [3, 128, 2048], P(None, ('groups', 'tiles'), ('band', 'stokes')), parts along dimension 1, may hold values from -4 to 4
- noise_block: float32 [6, 128, 2048], P(None, ('groups', 'tiles'), ('band', 'stokes')), parts along dimension 1, may hold values from -0.09 to 0.4, as said below
- edges: float32 [2, 128, 2048], P(None, ('groups', 'tiles'), ('band', 'stokes')), parts along dimension 1, may hold values from 0.5 to 2
Outputs:
- correction: float32 [3, 128, 2048], P(None, ('groups', 'tiles'), ('band', 'stokes')), parts along dimension 1
The draws below stay inside these ranges and needn't reach their ends.
There are 2 independent parts, one for each index of `groups`. The reference program is written for one: setup_inputs(seed, part) draws one part's arguments, and reference() takes and returns one part's arrays. A program takes and returns all parts, laid end to end along the dimension named above; each array names one. Nothing has to cross between parts.
Inputs may be any that keep to these rules, and one draw needn't show every extreme that they name: `noise_block`: entries 0 to 2 are positive and each exceeds the sum of the magnitudes of the two couplings in its row of the 3 x 3 matrix.
All inputs are finite; a program needn't handle non-finite values.
Results may differ from the reference program's by a relative error of at most 0.00002.
Values sent between devices are 32-bit elements; how exact they have to be, the bound alone decides.
A program may use at most 64 MiB of HBM per device.

```python
import math
import jax
import jax.numpy as jnp

LEVELS = 5
PRE = 2
POST = 2
COARSE_SWEEPS = 8
NR = 64
NC = 2048


def draw_right_side(key, part):
    return jnp.clip(jax.random.normal(key, (3, NR, NC), jnp.float32), -4.0, 4.0)


def draw_noise_block(key, part):
    hits_key = jax.random.fold_in(key, 11)
    diag_key = jax.random.fold_in(key, 12)
    cross_key = jax.random.fold_in(key, 13)
    hits = jnp.exp(jax.random.uniform(hits_key, (1, NR, NC), jnp.float32, math.log(0.005), math.log(0.2)))
    diagonal = hits * jax.random.uniform(diag_key, (3, NR, NC), jnp.float32, 1.0, 2.0)
    crossed = hits * jax.random.uniform(cross_key, (3, NR, NC), jnp.float32, -0.45, 0.45)
    return jnp.concatenate([diagonal, crossed], axis=0)


def shard_levels(stream_key, extent, pieces, least, high):
    def one(dim, parts):
        draws = jax.random.uniform(jax.random.fold_in(jax.random.fold_in(stream_key, 6), dim), (parts,), jnp.float32, least / len(pieces), high / len(pieces))
        return jnp.repeat(jnp.exp(draws), extent[dim] // parts).reshape((-1,) + (1,) * (len(extent) - dim - 1))

    loudness = one(*pieces[0])
    for cut in pieces[1:]:
        loudness = loudness * one(*cut)
    return loudness


def setup_inputs(seed: int = 0, part: int = 0) -> dict:
    seeds = jax.random.split(jax.random.key(seed), 4)
    part_keys = jax.random.split(jax.random.fold_in(seeds[3], part), 4)
    return {
        "right_side": draw_right_side(jax.random.fold_in(jax.random.fold_in(seeds[3], part), 71), part),
        "noise_block": draw_noise_block(jax.random.fold_in(jax.random.fold_in(seeds[3], part), 71), part),
        "edges": jnp.clip(jnp.exp(math.log(2.0) - 1.3862944 * jax.random.uniform(part_keys[2], (2, NR, NC), jnp.float32) ** shard_levels(part_keys[2], (2, NR, NC), ((1, 4), (2, 4)), -0.2, 0.2)), 0.5, 2.0),
    }


OMEGA = 0.8


def apply_padded(iterate, padded, noise, couplings):
    first = noise[0] * iterate[0] + noise[3] * iterate[1] + noise[4] * iterate[2]
    second = noise[3] * iterate[0] + noise[1] * iterate[1] + noise[5] * iterate[2]
    third = noise[4] * iterate[0] + noise[5] * iterate[1] + noise[2] * iterate[2]
    totals = couplings[0] + couplings[1] + couplings[2] + couplings[3]
    neighbours = (couplings[0] * padded[:, 2:, 1:-1] + couplings[1] * padded[:, :-2, 1:-1]
                  + couplings[2] * padded[:, 1:-1, 2:] + couplings[3] * padded[:, 1:-1, :-2])
    return jnp.stack([first, second, third]) + totals * iterate - neighbours


def zero_rim(iterate):
    return jnp.pad(iterate, ((0, 0), (1, 1), (1, 1)))


def diagonal_of(noise, couplings):
    return noise[0:3] + (couplings[0] + couplings[1] + couplings[2] + couplings[3])


def restrict_sum(field):
    depth, height, width = field.shape
    return field.reshape(depth, height // 2, 2, width // 2, 2).sum(axis=(2, 4))


def coarsen_couplings(couplings):
    depth, height, width = couplings.shape
    blocks = couplings.reshape(4, height // 2, 2, width // 2, 2)
    downward = blocks[0][:, 1, :, :].sum(axis=-1)
    upward = blocks[1][:, 0, :, :].sum(axis=-1)
    rightward = blocks[2][:, :, :, 1].sum(axis=1)
    leftward = blocks[3][:, :, :, 0].sum(axis=1)
    return jnp.stack([downward, upward, rightward, leftward])


def prolong(coarse):
    return jnp.repeat(jnp.repeat(coarse, 2, axis=1), 2, axis=2)


def smooth(iterate, source, noise, couplings, diagonal):
    image = apply_padded(iterate, zero_rim(iterate), noise, couplings)
    return iterate + OMEGA * (source - image) / diagonal


def cycle(source, noise, couplings, level_index):
    diagonal = diagonal_of(noise, couplings)
    iterate = OMEGA * source / diagonal
    if level_index == LEVELS - 1:
        for sweep_index in range(COARSE_SWEEPS - 1):
            iterate = smooth(iterate, source, noise, couplings, diagonal)
        return iterate
    for sweep_index in range(PRE - 1):
        iterate = smooth(iterate, source, noise, couplings, diagonal)
    residual = source - apply_padded(iterate, zero_rim(iterate), noise, couplings)
    coarse = cycle(restrict_sum(residual), restrict_sum(noise), coarsen_couplings(couplings), level_index + 1)
    iterate = iterate + prolong(coarse)
    for sweep_index in range(POST):
        iterate = smooth(iterate, source, noise, couplings, diagonal)
    return iterate


def reference(right_side, noise_block, edges):
    upward = jnp.pad(edges[0], ((1, 0), (0, 0)))[:-1, :]
    leftward = jnp.pad(edges[1], ((0, 0), (1, 0)))[:, :-1]
    couplings = jnp.stack([edges[0], upward, edges[1], leftward])
    return cycle(right_side, noise_block, couplings, 0)
```

```python
import functools

import jax
import jax.numpy as jnp
from jax import lax
from jax.experimental import pallas as pl
from jax.experimental.pallas import tpu as pltpu
from jax.sharding import PartitionSpec as P

OMEGA = 0.8
COARSE_SWEEPS = 8
HALO = 8
SIDE = 128
MESH = pl.DeviceIdType.MESH
F32 = jnp.float32


def dot(x, y):
    return jnp.dot(x, y, precision=lax.Precision.HIGHEST, preferred_element_type=F32)


def iota(shape, dim):
    return lax.broadcasted_iota(jnp.int32, shape, dim)


def pool_matrix(n, m, off=0, odd=False):
    c, j = iota((n, m), 0), iota((n, m), 1)
    hit = c == 2 * j + 1 + off
    if not odd:
        hit = hit | (c == 2 * j + off)
    return jnp.where(hit, 1.0, 0.0).astype(F32)


def spread_matrix(n, m, off=0):
    c, j = iota((n, m), 0), iota((n, m), 1)
    low = 2 * (c - off)
    return jnp.where((j == low) | (j == low + 1), 1.0, 0.0).astype(F32)


def chunks(a):
    return range(a.shape[1] // 8)


def setup(a, aux):
    for q in chunks(a):
        rows = slice(8 * q, 8 * q + 8)
        down, right = a[9, rows], a[10, rows]
        if q == 0:
            up = jnp.where(iota(down.shape, 0) == 0, 0.0, pltpu.roll(down, 1, 0))
        else:
            up = a[9, 8 * q - 1 : 8 * q + 7]
        left = pltpu.roll(right, 1, 1)
        total = down + up + right + left
        aux[0, rows], aux[1, rows], aux[2, rows] = up, left, total
        for k in range(3):
            aux[3 + k, rows] = jnp.where(down > 0, OMEGA / (a[3 + k, rows] + total), 0.0)


def first(a, aux, v):
    for q in chunks(a):
        rows = slice(8 * q, 8 * q + 8)
        for k in range(3):
            v[k, 8 + 8 * q : 16 + 8 * q] = aux[3 + k, rows] * a[k, rows]


def residual_at(a, aux, v, q):
    rows = slice(8 * q, 8 * q + 8)
    mid = [v[k, 8 + 8 * q : 16 + 8 * q] for k in range(3)]
    n = [a[3 + i, rows] for i in range(6)]
    down, right, up, left, total = a[9, rows], a[10, rows], aux[0, rows], aux[1, rows], aux[2, rows]
    width = mid[0].shape[1]
    image = [
        n[0] * mid[0] + n[3] * mid[1] + n[4] * mid[2],
        n[3] * mid[0] + n[1] * mid[1] + n[5] * mid[2],
        n[4] * mid[0] + n[5] * mid[1] + n[2] * mid[2],
    ]
    out = []
    for k in range(3):
        near = (
            down * v[k, 9 + 8 * q : 17 + 8 * q]
            + up * v[k, 7 + 8 * q : 15 + 8 * q]
            + right * pltpu.roll(mid[k], width - 1, 1)
            + left * pltpu.roll(mid[k], 1, 1)
        )
        out.append(a[k, rows] - (image[k] + total * mid[k] - near))
    return mid, out


def sweep(a, aux, src, dst, which=None):
    for q in chunks(a) if which is None else which:
        mid, res = residual_at(a, aux, src, q)
        for k in range(3):
            dst[k, 8 + 8 * q : 16 + 8 * q] = mid[k] + aux[3 + k, 8 * q : 8 * q + 8] * res[k]


def residual(a, aux, v, r):
    height = a.shape[1]
    for q in chunks(a):
        _, res = residual_at(a, aux, v, q)
        for k in range(3):
            r[k * height + 8 * q : k * height + 8 * q + 8, :] = res[k]


def pool_lanes(x, matrix):
    n = matrix.shape[0]
    width = x.shape[1]
    parts = []
    for b in range(0, width, n):
        if b + n <= width:
            parts.append(dot(x[:, b : b + n], matrix))
        else:
            parts.append(dot(x[:, b:width], matrix[: width - b]))
    return parts


def pool_rows(parts, st, odd=False):
    out = []
    for b, part in enumerate(parts):
        n = part.shape[0]
        st[b, 0:n, :] = part
        top = st[b, pl.ds(1, n // 2, stride=2), :]
        out.append(top if odd else top + st[b, pl.ds(0, n // 2, stride=2), :])
    return out


def coarsen_coefficients(arrays, st, even, odd):
    noise = pool_rows(pool_lanes(jnp.concatenate(arrays[:6], 0), even), st)
    down = pool_rows(pool_lanes(arrays[6], even), st, odd=True)
    right = pool_rows(pool_lanes(arrays[7], odd), st)
    h = arrays[0].shape[0] // 2
    out = []
    for i in range(6):
        out.append([p[i * h : i * h + h] for p in noise])
    return out + [down, right]


def spread_rows(parts, st):
    for b, part in enumerate(parts):
        n = part.shape[0]
        st[b, pl.ds(0, n, stride=2), :] = part
        st[b, pl.ds(1, n, stride=2), :] = part


def put(a, channel, row, parts):
    for b, part in enumerate(parts):
        a[channel, row : row + part.shape[0], SIDE * b : SIDE * b + SIDE] = part


def add_spread(v, dst, st, stride, blocks, height, row0=0):
    for k in range(3):
        for b in range(blocks):
            lanes = slice(SIDE * b, SIDE * b + SIDE)
            dst[k, 8 : 8 + height, lanes] = v[k, 8 : 8 + height, lanes] + st[b, stride * k + row0 : stride * k + row0 + height, :]


def kernel(
    T, NB, NS, rhs, noise, edges, out,
    a0, x0, u0, w0, r0, a1, x1, u1, w1, r1, a2, x2, u2, w2, r2, a3, x3, u3, w3, r3, a4, x4, u4, w4,
    st, win, coef_slots, src_slots, side_rows,
    in_sem, halo_send, halo_recv, coef_send, coef_recv, src_send, src_recv, row_send, row_recv,
):
    t = lax.axis_index("tiles")
    col = lax.axis_index("band") * NS + lax.axis_index("stokes")
    cols = NB * NS
    h, w = rhs.shape[1], rhs.shape[2]
    has = {-1: col > 0, 0: None, 1: col < cols - 1}
    rowhas = {-1: t > 0, 0: None, 1: t < T - 1}

    def when(*conds):
        conds = [c for c in conds if c is not None]
        if not conds:
            return lambda f: f()
        return pl.when(functools.reduce(jnp.logical_and, conds))

    def device(tile, dc):
        c = col + dc
        return {"tiles": tile, "band": c // NS, "stokes": lax.rem(c, NS)}

    own_rows, own_cols = slice(HALO, HALO + h), slice(SIDE, SIDE + w)
    loads = [
        pltpu.make_async_copy(rhs, a0.at[0:3, own_rows, own_cols], in_sem.at[0]),
        pltpu.make_async_copy(noise, a0.at[3:9, own_rows, own_cols], in_sem.at[1]),
        pltpu.make_async_copy(edges, a0.at[9:11, own_rows, own_cols], in_sem.at[2]),
    ]
    for c in loads:
        c.start()

    partners = [(dt, dc) for dc in (-1, 0, 1) for dt in range(T) if dt or dc]
    barrier = pltpu.get_barrier_semaphore()
    for dt, dc in partners:
        @when(has[dc])
        def _(dt=dt, dc=dc):
            pl.semaphore_signal(barrier, inc=1, device_id=device(lax.rem(t + dt, T), dc), device_id_type=MESH)

    @pl.when(t == 0)
    def _():
        a0[:, 0:HALO, :] = jnp.zeros_like(a0[:, 0:HALO, :])
        side_rows[0] = jnp.zeros_like(side_rows[0])

    @pl.when(t == T - 1)
    def _():
        a0[:, HALO + h :, :] = jnp.zeros_like(a0[:, HALO + h :, :])
        side_rows[1] = jnp.zeros_like(side_rows[1])

    @pl.when(col == 0)
    def _():
        a0[:, :, 0:SIDE] = jnp.zeros_like(a0[:, :, 0:SIDE])
        for s in range(T):
            coef_slots[s, 0] = jnp.zeros_like(coef_slots[s, 0])
            src_slots[s, 0] = jnp.zeros_like(src_slots[s, 0])

    @pl.when(col == cols - 1)
    def _():
        a0[:, :, SIDE + w :] = jnp.zeros_like(a0[:, :, SIDE + w :])
        for s in range(T):
            coef_slots[s, 2] = jnp.zeros_like(coef_slots[s, 2])
            src_slots[s, 2] = jnp.zeros_like(src_slots[s, 2])

    for a in (a1, a3, a4):
        a[...] = jnp.zeros_like(a)
    for v in (x0, u0, x1, u1, x2, u2, x3, u3, x4, u4):
        v[:, 0:8, :] = jnp.zeros_like(v[:, 0:8, :])
        n = v.shape[1]
        v[:, n - 8 : n, :] = jnp.zeros_like(v[:, n - 8 : n, :])

    sides = 1 + jnp.where(col > 0, 1, 0) + jnp.where(col < cols - 1, 1, 0)
    pl.semaphore_wait(barrier, sides * T - 1)
    for c in loads:
        c.wait()

    row_src = {-1: slice(HALO, 2 * HALO), 0: own_rows, 1: slice(h, HALO + h)}
    row_dst = {-1: slice(HALO + h, 2 * HALO + h), 0: own_rows, 1: slice(0, HALO)}
    col_src = {-1: slice(SIDE, 2 * SIDE), 0: own_cols, 1: slice(w, SIDE + w)}
    col_dst = {-1: slice(SIDE + w, 2 * SIDE + w), 0: own_cols, 1: slice(0, SIDE)}

    def halo(dr, dc):
        i = (dr + 1) * 3 + dc + 1
        return pltpu.make_async_remote_copy(
            src_ref=a0.at[:, row_src[dr], col_src[dc]],
            dst_ref=a0.at[:, row_dst[dr], col_dst[dc]],
            send_sem=halo_send.at[i],
            recv_sem=halo_recv.at[i],
            device_id=device(t + dr, dc),
            device_id_type=MESH,
        )

    ways = [(-1, 0), (1, 0), (-1, -1), (-1, 1), (1, -1), (1, 1), (0, -1), (0, 1)]
    for dr, dc in ways:
        @when(rowhas[dr], has[dc])
        def _(dr=dr, dc=dc):
            halo(dr, dc).start()

    def gather(slots, send, recv, dt, dc):
        return pltpu.make_async_remote_copy(
            src_ref=slots.at[t, 1],
            dst_ref=slots.at[t, 1 - dc],
            send_sem=send.at[dt, dc + 1],
            recv_sem=recv.at[t, 1 - dc],
            device_id=device(lax.rem(t + dt, T), dc),
            device_id_type=MESH,
        )

    def arrival(slots, send, recv, dt, dc):
        s = lax.rem(t + dt, T)
        return pltpu.make_async_remote_copy(
            src_ref=slots.at[s, dc + 1],
            dst_ref=slots.at[s, dc + 1],
            send_sem=send.at[dt, dc + 1],
            recv_sem=recv.at[s, dc + 1],
            device_id=device(s, dc),
            device_id_type=MESH,
        )

    even, odd = pool_matrix(256, 128), pool_matrix(256, 128, odd=True)
    wide = spread_matrix(128, 256)

    fine = [a0[3 + i, own_rows, own_cols] for i in range(8)]
    mid = coarsen_coefficients(fine, st, even, odd)
    mid = [jnp.concatenate(parts, 1) for parts in mid]
    low = [parts[0] for parts in coarsen_coefficients(mid, st, even, odd)]
    coef_slots[t, 1] = jnp.concatenate(low, 0)
    for dt, dc in partners:
        @when(has[dc])
        def _(dt=dt, dc=dc):
            gather(coef_slots, coef_send, coef_recv, dt, dc).start()

    for dr, dc in ways:
        @when(rowhas[dr], has[dc])
        def _(dr=dr, dc=dc):
            halo(-dr, -dc).wait_recv()

    setup(a0, w0)
    first(a0, w0, x0)
    sweep(a0, w0, x0, u0)
    residual(a0, w0, u0, r0)
    source = pool_rows(pool_lanes(r0[...], even), st)
    h1 = a0.shape[1] // 2
    for k in range(3):
        put(a1, k, 4, [p[k * h1 : k * h1 + h1] for p in source])
    wider = coarsen_coefficients([a0[3 + i] for i in range(8)], st, even, odd)
    for i in range(8):
        put(a1, 3 + i, 4, wider[i])

    setup(a1, w1)
    first(a1, w1, x1)
    sweep(a1, w1, x1, u1)
    residual(a1, w1, u1, r1)
    own = dot(r1[...], pool_matrix(384, 128, off=64))
    source = pool_rows([own], st)[0]
    packed = [source[12 * k + 4 : 12 * k + 8] for k in range(3)]
    src_slots[t, 1] = jnp.concatenate(packed + [jnp.zeros((4, SIDE), F32)], 0)
    for dt, dc in partners:
        @when(has[dc])
        def _(dt=dt, dc=dc):
            gather(src_slots, src_send, src_recv, dt, dc).start()

    def rows_copy(dr):
        i = (dr + 1) // 2
        return pltpu.make_async_remote_copy(
            src_ref=u1.at[:, 16:24, :],
            dst_ref=side_rows.at[1 - i],
            send_sem=row_send.at[i],
            recv_sem=row_recv.at[1 - i],
            device_id=device(t + dr, 0),
            device_id_type=MESH,
        )

    for dr in (-1, 1):
        @when(rowhas[dr])
        def _(dr=dr):
            rows_copy(dr).start()

    def assemble(slots, recv, send, channel, count):
        for dt, dc in partners:
            @when(has[dc])
            def _(dt=dt, dc=dc):
                arrival(slots, send, recv, dt, dc).wait_recv()
        for j in range(T // 2):
            for c in range(3):
                one, two = slots[2 * j, c], slots[2 * j + 1, c]
                for i in range(count):
                    a2[channel + i, 8 * j : 8 * j + 8, SIDE * c : SIDE * c + SIDE] = jnp.concatenate(
                        [one[4 * i : 4 * i + 4], two[4 * i : 4 * i + 4]], 0
                    )

    assemble(coef_slots, coef_recv, coef_send, 3, 8)
    setup(a2, w2)
    for a, b, aux in ((a2, a3, w3), (a3, a4, w4)):
        for i, parts in enumerate(coarsen_coefficients([a[3 + i] for i in range(8)], st, even, odd)):
            put(b, 3 + i, 0, parts)
        setup(b, aux)
    assemble(src_slots, src_recv, src_send, 0, 3)

    for a, aux, x, u, r, b in ((a2, w2, x2, u2, r2, a3), (a3, w3, x3, u3, r3, a4)):
        first(a, aux, x)
        sweep(a, aux, x, u)
        residual(a, aux, u, r)
        source = pool_rows(pool_lanes(r[...], even), st)
        half = a.shape[1] // 2
        for k in range(3):
            put(b, k, 0, [p[k * half : k * half + half] for p in source])
    first(a4, w4, x4)
    now, then = x4, u4
    for _ in range(COARSE_SWEEPS - 1):
        sweep(a4, w4, now, then)
        now, then = then, now
    coarse = now
    for a, aux, x, u in ((a3, w3, x3, u3), (a2, w2, x2, u2)):
        n = coarse.shape[1] - 16
        y = jnp.concatenate([coarse[k, 8 : 8 + n] for k in range(3)], 0)
        parts = []
        for b in range(y.shape[1] // 128):
            z = dot(y[:, 128 * b : 128 * b + 128], wide)
            parts += [z[:, :128], z[:, 128:]]
        parts = parts[: a.shape[2] // 128]
        spread_rows(parts, st)
        add_spread(u, x, st, 2 * n, len(parts), a.shape[1])
        sweep(a, aux, x, u)
        sweep(a, aux, u, x)
        coarse = x

    for s in range(T):
        @pl.when(t == s)
        def _(s=s):
            for k in range(3):
                win[16 * k : 16 * k + 16, :] = x2[k, 4 + 4 * s : 20 + 4 * s]
    y = dot(win[...], spread_matrix(384, 384, off=96))
    spread_rows([y[:, 128 * b : 128 * b + 128] for b in range(3)], st)
    for dr in (-1, 1):
        @when(rowhas[dr])
        def _(dr=dr):
            rows_copy(dr).wait_send()
            rows_copy(-dr).wait_recv()
    u1[:, 8:16, :] = side_rows[0]
    u1[:, 24:32, :] = side_rows[1]
    add_spread(u1, x1, st, 32, 3, 24)
    sweep(a1, w1, x1, u1)
    sweep(a1, w1, u1, x1)

    y = jnp.concatenate([x1[k, 8:32] for k in range(3)], 0)
    parts = []
    for b in range(3):
        z = dot(y[:, 128 * b : 128 * b + 128], wide)
        parts += [z[:, :128], z[:, 128:]]
    spread_rows(parts, st)
    add_spread(u0, x0, st, 48, 6, 32, row0=8)
    sweep(a0, w0, x0, u0)
    for q in range(1, 1 + h // 8):
        mid, res = residual_at(a0, w0, u0, q)
        for k in range(3):
            new = mid[k] + w0[3 + k, 8 * q : 8 * q + 8] * res[k]
            out[k, 8 * q - 8 : 8 * q, :] = new[:, own_cols]

    for dr, dc in ways:
        @when(rowhas[dr], has[dc])
        def _(dr=dr, dc=dc):
            halo(dr, dc).wait_send()
    for dt, dc in partners:
        @when(has[dc])
        def _(dt=dt, dc=dc):
            gather(coef_slots, coef_send, coef_recv, dt, dc).wait_send()
            gather(src_slots, src_send, src_recv, dt, dc).wait_send()


def on_device(right_side, noise_block, edges):
    T, NB, NS = lax.axis_size("tiles"), lax.axis_size("band"), lax.axis_size("stokes")
    _, h, w = right_side.shape
    shapes = [
        (h + 2 * HALO, w + 2 * SIDE),
        (h // 2 + 16, w // 2 + SIDE),
        (h // 4 * T, 3 * SIDE),
        (max(8, h // 8 * T), 2 * SIDE),
        (max(8, h // 16 * T), SIDE),
    ]
    scratch = []
    for i, (n, m) in enumerate(shapes):
        scratch += [
            pltpu.VMEM((11, n, m), F32),
            pltpu.VMEM((3, n + 16, m), F32),
            pltpu.VMEM((3, n + 16, m), F32),
            pltpu.VMEM((6, n, m), F32),
        ]
        if i < 4:
            scratch.append(pltpu.VMEM((3 * n, m), F32))
    scratch += [
        pltpu.VMEM((6, max(8 * 32, 6 * h // 4 * T), SIDE), F32),
        pltpu.VMEM((48, 3 * SIDE), F32),
        pltpu.VMEM((T, 3, 32, SIDE), F32),
        pltpu.VMEM((T, 3, 16, SIDE), F32),
        pltpu.VMEM((2, 3, 8, 3 * SIDE), F32),
        pltpu.SemaphoreType.DMA((3,)),
        pltpu.SemaphoreType.DMA((9,)),
        pltpu.SemaphoreType.DMA((9,)),
        pltpu.SemaphoreType.DMA((T, 3)),
        pltpu.SemaphoreType.DMA((T, 3)),
        pltpu.SemaphoreType.DMA((T, 3)),
        pltpu.SemaphoreType.DMA((T, 3)),
        pltpu.SemaphoreType.DMA((2,)),
        pltpu.SemaphoreType.DMA((2,)),
    ]
    return pl.pallas_call(
        functools.partial(kernel, T, NB, NS),
        out_shape=jax.ShapeDtypeStruct(right_side.shape, F32),
        in_specs=[pl.BlockSpec(memory_space=pl.ANY)] * 3,
        out_specs=pl.BlockSpec(memory_space=pltpu.VMEM),
        scratch_shapes=scratch,
        compiler_params=pltpu.CompilerParams(
            collective_id=0, has_side_effects=True, vmem_limit_bytes=40 * 1024 * 1024
        ),
    )(right_side, noise_block, edges)


def solution(mesh):
    spec = P(None, ("groups", "tiles"), ("band", "stokes"))
    return jax.shard_map(
        on_device, mesh=mesh, in_specs=(spec, spec, spec), out_specs=spec, check_vma=False
    )
```

```python
import functools

import jax
import jax.numpy as jnp
from jax import lax
from jax.experimental import pallas as pl
from jax.experimental.pallas import tpu as pltpu
from jax.sharding import PartitionSpec as P

OMEGA = 0.8
COARSE_SWEEPS = 8
HALO = 8
SIDE = 128
DEEP = 11
MESH = pl.DeviceIdType.MESH
F32 = jnp.float32


def rounded(x):
    return x.astype(jnp.bfloat16).astype(F32)


def dot(x, y):
    n = x.shape[0]
    high = rounded(x)
    rest = x - high
    mid = rounded(rest)
    pieces = jnp.concatenate([high, mid, rest - mid], 0)
    z = jnp.dot(pieces, y, precision=lax.Precision.DEFAULT, preferred_element_type=F32)
    return z[:n] + (z[n : 2 * n] + z[2 * n :])


def iota(shape, dim):
    return lax.broadcasted_iota(jnp.int32, shape, dim)


def ones(hit):
    return jnp.where(hit, 1.0, 0.0).astype(F32)


def half(i):
    return lax.shift_right_logical(i, 1)


def pool_matrix(n, m, odd=False):
    c, j = iota((n, m), 0), iota((n, m), 1)
    hit = c == 2 * j + 1
    return ones(hit if odd else hit | (c == 2 * j))


def spread_matrix(n, m):
    c, j = iota((n, m), 0), iota((n, m), 1)
    return ones(c == half(j))


def ring_pool(odd=False):
    c, j = iota((SIDE, SIDE), 0), iota((SIDE, SIDE), 1)
    hit = j == half(c) + jnp.where(c >= 64, 64, 0)
    return ones(hit & ((c & 1) == 1) if odd else hit)


def ring_spread():
    c, j = iota((SIDE, SIDE), 0), iota((SIDE, SIDE), 1)
    return ones(c == half(j) + jnp.where(j >= 64, 64, 0))


def ring_from_blocks(n):
    c, j = iota((n, n), 0), iota((n, n), 1)
    return ones(c == half(j) + jnp.where(j >= 320, -64, 128))


def chunks(a):
    return range(a.shape[1] // 8)


def setup(a, aux):
    for q in chunks(a):
        rows = slice(8 * q, 8 * q + 8)
        down, right = a[9, rows], a[10, rows]
        if q == 0:
            up = jnp.where(iota(down.shape, 0) == 0, 0.0, pltpu.roll(down, 1, 0))
        else:
            up = a[9, 8 * q - 1 : 8 * q + 7]
        left = pltpu.roll(right, 1, 1)
        total = down + up + right + left
        aux[0, rows], aux[1, rows], aux[2, rows] = up, left, total
        for k in range(3):
            aux[3 + k, rows] = jnp.where(down > 0, OMEGA / (a[3 + k, rows] + total), 0.0)


def first(a, aux, v):
    for q in chunks(a):
        rows = slice(8 * q, 8 * q + 8)
        for k in range(3):
            v[k, 8 + 8 * q : 16 + 8 * q] = aux[3 + k, rows] * a[k, rows]


def residual_at(a, aux, v, q):
    rows = slice(8 * q, 8 * q + 8)
    mid = [v[k, 8 + 8 * q : 16 + 8 * q] for k in range(3)]
    n = [a[3 + i, rows] for i in range(6)]
    down, right, up, left, total = a[9, rows], a[10, rows], aux[0, rows], aux[1, rows], aux[2, rows]
    width = mid[0].shape[1]
    image = [
        n[0] * mid[0] + n[3] * mid[1] + n[4] * mid[2],
        n[3] * mid[0] + n[1] * mid[1] + n[5] * mid[2],
        n[4] * mid[0] + n[5] * mid[1] + n[2] * mid[2],
    ]
    out = []
    for k in range(3):
        near = (
            down * v[k, 9 + 8 * q : 17 + 8 * q]
            + up * v[k, 7 + 8 * q : 15 + 8 * q]
            + right * pltpu.roll(mid[k], width - 1, 1)
            + left * pltpu.roll(mid[k], 1, 1)
        )
        out.append(a[k, rows] - (image[k] + total * mid[k] - near))
    return mid, out


def sweep(a, aux, src, dst, which=None):
    for q in chunks(a) if which is None else which:
        mid, res = residual_at(a, aux, src, q)
        for k in range(3):
            dst[k, 8 + 8 * q : 16 + 8 * q] = mid[k] + aux[3 + k, 8 * q : 8 * q + 8] * res[k]


def residual(a, aux, v, r):
    height = a.shape[1]
    for q in chunks(a):
        _, res = residual_at(a, aux, v, q)
        for k in range(3):
            r[k * height + 8 * q : k * height + 8 * q + 8, :] = res[k]


def pool_lanes(x, matrix, tail=None):
    n = matrix.shape[0]
    width = x.shape[1]
    parts = []
    for b in range(0, width, n):
        if b + n <= width:
            parts.append(dot(x[:, b : b + n], matrix))
        else:
            parts.append(dot(x[:, b:width], matrix[: width - b] if tail is None else tail))
    return parts


def pool_rows(parts, st, odd=False):
    out = []
    for b, part in enumerate(parts):
        n = part.shape[0]
        st[b, 0:n, :] = part
        top = st[b, pl.ds(1, n // 2, stride=2), :]
        out.append(top if odd else top + st[b, pl.ds(0, n // 2, stride=2), :])
    return out


def coarsen_coefficients(arrays, st, even, odd):
    h = arrays[0].shape[0]
    parts = pool_lanes(jnp.concatenate(arrays[:7], 0), even)
    noise = pool_rows([p[: 6 * h] for p in parts], st)
    down = pool_rows([p[6 * h :] for p in parts], st, odd=True)
    right = pool_rows(pool_lanes(arrays[7], odd), st)
    h = h // 2
    out = []
    for i in range(6):
        out.append([p[i * h : i * h + h] for p in noise])
    return out + [down, right]


def spread_rows(parts, st):
    for b, part in enumerate(parts):
        n = part.shape[0]
        st[b, pl.ds(0, n, stride=2), :] = part
        st[b, pl.ds(1, n, stride=2), :] = part


def put(a, channel, row, parts, tile=0):
    for b, part in enumerate(parts, tile):
        a[channel, row : row + part.shape[0], SIDE * b : SIDE * b + SIDE] = part


def add_spread(v, dst, st, stride, blocks, height, row0=0):
    for k in range(3):
        for b in range(blocks):
            lanes = slice(SIDE * b, SIDE * b + SIDE)
            dst[k, 8 : 8 + height, lanes] = v[k, 8 : 8 + height, lanes] + st[b, stride * k + row0 : stride * k + row0 + height, :]


def kernel(
    T, NB, NS, rhs, noise, edges, out,
    a0, x0, u0, w0, r0, a1, x1, u1, w1, r1, a2, x2, u2, w2, r2, a3, x3, u3, w3, r3, a4, x4, u4, w4,
    st, win, sent, got, coef_slots, src_slots, side_rows,
    in_sem, halo_send, halo_recv, coef_send, coef_recv, src_send, src_recv, row_send, row_recv,
):
    t = lax.axis_index("tiles")
    col = lax.axis_index("band") * NS + lax.axis_index("stokes")
    cols = NB * NS
    h, w = rhs.shape[1], rhs.shape[2]
    has = {-1: col > 0, 0: None, 1: col < cols - 1}
    rowhas = {-1: t > 0, 0: None, 1: t < T - 1}

    def when(*conds):
        conds = [c for c in conds if c is not None]
        if not conds:
            return lambda f: f()
        return pl.when(functools.reduce(jnp.logical_and, conds))

    def device(tile, dc):
        c = col + dc
        return {"tiles": tile, "band": c // NS, "stokes": lax.rem(c, NS)}

    own_rows, own_cols = slice(HALO, HALO + h), slice(0, w)
    loads = [
        pltpu.make_async_copy(rhs, a0.at[0:3, own_rows, own_cols], in_sem.at[0]),
        pltpu.make_async_copy(noise, a0.at[3:9, own_rows, own_cols], in_sem.at[1]),
        pltpu.make_async_copy(edges, a0.at[9:11, own_rows, own_cols], in_sem.at[2]),
    ]
    for c in loads:
        c.start()

    partners = [(dt, dc) for dc in (-1, 0, 1) for dt in range(T) if dt or dc]
    barrier = pltpu.get_barrier_semaphore()
    for dt, dc in partners:
        @when(has[dc])
        def _(dt=dt, dc=dc):
            pl.semaphore_signal(barrier, inc=1, device_id=device(lax.rem(t + dt, T), dc), device_id_type=MESH)

    @pl.when(t == 0)
    def _():
        a0[:, 0:HALO, own_cols] = jnp.zeros_like(a0[:, 0:HALO, own_cols])
        got[:, 0:HALO] = jnp.zeros_like(got[:, 0:HALO])
        side_rows[0] = jnp.zeros_like(side_rows[0])

    @pl.when(t == T - 1)
    def _():
        a0[:, HALO + h :, own_cols] = jnp.zeros_like(a0[:, HALO + h :, own_cols])
        got[:, HALO + h :] = jnp.zeros_like(got[:, HALO + h :])
        side_rows[1] = jnp.zeros_like(side_rows[1])

    @pl.when(col == 0)
    def _():
        got[0] = jnp.zeros_like(got[0])
        for s in range(T):
            coef_slots[s, 0] = jnp.zeros_like(coef_slots[s, 0])
            src_slots[s, 0] = jnp.zeros_like(src_slots[s, 0])

    @pl.when(col == cols - 1)
    def _():
        got[1] = jnp.zeros_like(got[1])
        for s in range(T):
            coef_slots[s, 2] = jnp.zeros_like(coef_slots[s, 2])
            src_slots[s, 2] = jnp.zeros_like(src_slots[s, 2])

    for a in (a1, a3, a4):
        a[...] = jnp.zeros_like(a)
    for v in (x0, u0, x1, u1, x2, u2, x3, u3, x4, u4):
        v[:, 0:8, :] = jnp.zeros_like(v[:, 0:8, :])
        n = v.shape[1]
        v[:, n - 8 : n, :] = jnp.zeros_like(v[:, n - 8 : n, :])

    for c in loads:
        c.wait()

    lane = iota((8, SIDE), 1)
    for q in range(h // 8):
        rows = slice(HALO + 8 * q, HALO + 8 * q + 8)
        head = tail = jnp.zeros((8, SIDE), F32)
        for i in range(11):
            here = (lane >= DEEP * i) & (lane < DEEP * i + DEEP)
            one, two = a0[i, rows, 0:SIDE], a0[i, rows, w - SIDE : w]
            head = jnp.where(here, pltpu.roll(one, DEEP * i, 1) if i else one, head)
            tail = jnp.where(here, pltpu.roll(two, (DEEP * i + DEEP) % SIDE, 1), tail)
        sent[0, 8 * q : 8 * q + 8], sent[1, 8 * q : 8 * q + 8] = head, tail

    sides = 1 + jnp.where(col > 0, 1, 0) + jnp.where(col < cols - 1, 1, 0)
    pl.semaphore_wait(barrier, sides * T - 1)

    row_src = {-1: slice(HALO, 2 * HALO), 1: slice(h, HALO + h)}
    row_dst = {-1: slice(HALO + h, 2 * HALO + h), 0: own_rows, 1: slice(0, HALO)}
    part_src = {-1: slice(0, HALO), 0: slice(0, h), 1: slice(h - HALO, h)}

    def halo(dr, dc):
        i = (dr + 1) * 3 + dc + 1
        if dc:
            src = sent.at[(dc + 1) // 2, part_src[dr]]
            dst = got.at[(1 - dc) // 2, row_dst[dr]]
        else:
            src, dst = a0.at[:, row_src[dr], own_cols], a0.at[:, row_dst[dr], own_cols]
        return pltpu.make_async_remote_copy(
            src_ref=src,
            dst_ref=dst,
            send_sem=halo_send.at[i],
            recv_sem=halo_recv.at[i],
            device_id=device(t + dr, dc),
            device_id_type=MESH,
        )

    ways = [(0, -1), (0, 1), (-1, -1), (-1, 1), (1, -1), (1, 1), (-1, 0), (1, 0)]
    for dr, dc in ways:
        @when(rowhas[dr], has[dc])
        def _(dr=dr, dc=dc):
            halo(dr, dc).start()

    def gather(slots, send, recv, dt, dc):
        return pltpu.make_async_remote_copy(
            src_ref=slots.at[t, 1],
            dst_ref=slots.at[t, 1 - dc],
            send_sem=send.at[dt, dc + 1],
            recv_sem=recv.at[t, 1 - dc],
            device_id=device(lax.rem(t + dt, T), dc),
            device_id_type=MESH,
        )

    def arrival(slots, send, recv, dt, dc):
        s = lax.rem(t + dt, T)
        return pltpu.make_async_remote_copy(
            src_ref=slots.at[s, dc + 1],
            dst_ref=slots.at[s, dc + 1],
            send_sem=send.at[dt, dc + 1],
            recv_sem=recv.at[s, dc + 1],
            device_id=device(s, dc),
            device_id_type=MESH,
        )

    even, odd = pool_matrix(256, 128), pool_matrix(256, 128, odd=True)
    even_ring, odd_ring = ring_pool(), ring_pool(odd=True)
    wide = spread_matrix(128, 256)

    fine = [a0[3 + i, own_rows, own_cols] for i in range(8)]
    mid = coarsen_coefficients(fine, st, even, odd)
    for i in range(8):
        put(a1, 3 + i, 8, mid[i])
    mid = [jnp.concatenate(parts, 1) for parts in mid]
    low = [parts[0] for parts in coarsen_coefficients(mid, st, even, odd)]
    coef_slots[t, 1] = jnp.concatenate(low, 0)
    for dt, dc in partners:
        @when(has[dc])
        def _(dt=dt, dc=dc):
            gather(coef_slots, coef_send, coef_recv, dt, dc).start()

    for dr, dc in ways:
        @when(rowhas[dr], has[dc])
        def _(dr=dr, dc=dc):
            halo(-dr, -dc).wait_recv()

    for q in range(a0.shape[1] // 8):
        rows = slice(8 * q, 8 * q + 8)
        for i in range(11):
            right = pltpu.roll(got[1, rows], SIDE - DEEP * i, 1) if i else got[1, rows]
            left = pltpu.roll(got[0, rows], SIDE - DEEP - DEEP * i, 1)
            a0[i, rows, w : w + SIDE] = jnp.where(
                lane < DEEP, right, jnp.where(lane >= SIDE - DEEP, left, 0.0)
            )

    setup(a0, w0)
    first(a0, w0, x0)
    sweep(a0, w0, x0, u0)
    residual(a0, w0, u0, r0)
    source = pool_rows(pool_lanes(r0[...], even, even_ring), st)
    h1 = a0.shape[1] // 2
    for k in range(3):
        put(a1, k, 4, [p[k * h1 : k * h1 + h1] for p in source])
    beside = [
        jnp.concatenate([a0[3 + i, 0:HALO, own_cols], a0[3 + i, HALO + h :, own_cols]], 0) for i in range(8)
    ]
    for i, parts in enumerate(coarsen_coefficients(beside, st, even, odd)):
        put(a1, 3 + i, 4, [p[:4] for p in parts])
        put(a1, 3 + i, 16, [p[4:] for p in parts])
    ends = [a0[3 + i, :, w : w + SIDE] for i in range(8)]
    for i, parts in enumerate(coarsen_coefficients(ends, st, even_ring, odd_ring)):
        put(a1, 3 + i, 4, parts, 2)

    setup(a1, w1)
    first(a1, w1, x1)
    sweep(a1, w1, x1, u1)
    residual(a1, w1, u1, r1)
    own = dot(r1[:, 0:256], even)
    source = pool_rows([own], st)[0]
    packed = [source[12 * k + 4 : 12 * k + 8] for k in range(3)]
    src_slots[t, 1] = jnp.concatenate(packed + [jnp.zeros((4, SIDE), F32)], 0)
    for dt, dc in partners:
        @when(has[dc])
        def _(dt=dt, dc=dc):
            gather(src_slots, src_send, src_recv, dt, dc).start()

    def rows_copy(dr):
        i = (dr + 1) // 2
        return pltpu.make_async_remote_copy(
            src_ref=u1.at[:, 16:24, :],
            dst_ref=side_rows.at[1 - i],
            send_sem=row_send.at[i],
            recv_sem=row_recv.at[1 - i],
            device_id=device(t + dr, 0),
            device_id_type=MESH,
        )

    for dr in (-1, 1):
        @when(rowhas[dr])
        def _(dr=dr):
            rows_copy(dr).start()

    def assemble(slots, recv, send, channel, count):
        for dt, dc in partners:
            @when(has[dc])
            def _(dt=dt, dc=dc):
                arrival(slots, send, recv, dt, dc).wait_recv()
        for j in range(T // 2):
            for c in range(3):
                one, two = slots[2 * j, c], slots[2 * j + 1, c]
                for i in range(count):
                    a2[channel + i, 8 * j : 8 * j + 8, SIDE * c : SIDE * c + SIDE] = jnp.concatenate(
                        [one[4 * i : 4 * i + 4], two[4 * i : 4 * i + 4]], 0
                    )

    assemble(coef_slots, coef_recv, coef_send, 3, 8)
    setup(a2, w2)
    for a, b, aux in ((a2, a3, w3), (a3, a4, w4)):
        for i, parts in enumerate(coarsen_coefficients([a[3 + i] for i in range(8)], st, even, odd)):
            put(b, 3 + i, 0, parts)
        setup(b, aux)
    assemble(src_slots, src_recv, src_send, 0, 3)

    for a, aux, x, u, r, b in ((a2, w2, x2, u2, r2, a3), (a3, w3, x3, u3, r3, a4)):
        first(a, aux, x)
        sweep(a, aux, x, u)
        residual(a, aux, u, r)
        source = pool_rows(pool_lanes(r[...], even), st)
        n = a.shape[1] // 2
        for k in range(3):
            put(b, k, 0, [p[k * n : k * n + n] for p in source])
    first(a4, w4, x4)
    now, then = x4, u4
    for _ in range(COARSE_SWEEPS - 1):
        sweep(a4, w4, now, then)
        now, then = then, now
    coarse = now
    for a, aux, x, u in ((a3, w3, x3, u3), (a2, w2, x2, u2)):
        n = coarse.shape[1] - 16
        y = jnp.concatenate([coarse[k, 8 : 8 + n] for k in range(3)], 0)
        parts = []
        for b in range(y.shape[1] // 128):
            z = dot(y[:, 128 * b : 128 * b + 128], wide)
            parts += [z[:, :128], z[:, 128:]]
        parts = parts[: a.shape[2] // 128]
        spread_rows(parts, st)
        add_spread(u, x, st, 2 * n, len(parts), a.shape[1])
        sweep(a, aux, x, u)
        sweep(a, aux, u, x)
        coarse = x

    for s in range(T):
        @pl.when(t == s)
        def _(s=s):
            for k in range(3):
                win[16 * k : 16 * k + 16, :] = x2[k, 4 + 4 * s : 20 + 4 * s]
    y = dot(win[...], ring_from_blocks(384))
    spread_rows([y[:, 128 * b : 128 * b + 128] for b in range(3)], st)
    for dr in (-1, 1):
        @when(rowhas[dr])
        def _(dr=dr):
            rows_copy(dr).wait_send()
            rows_copy(-dr).wait_recv()
    u1[:, 8:16, :] = side_rows[0]
    u1[:, 24:32, :] = side_rows[1]
    add_spread(u1, x1, st, 32, 3, 24)
    sweep(a1, w1, x1, u1)
    sweep(a1, w1, u1, x1)

    y = jnp.concatenate([x1[k, 8:32] for k in range(3)], 0)
    parts = []
    for b in range(2):
        z = dot(y[:, 128 * b : 128 * b + 128], wide)
        parts += [z[:, :128], z[:, 128:]]
    parts.append(dot(y[:, 256:384], ring_spread()))
    spread_rows(parts, st)
    add_spread(u0, x0, st, 48, 5, 32, row0=8)
    sweep(a0, w0, x0, u0)
    for q in range(1, 1 + h // 8):
        mid, res = residual_at(a0, w0, u0, q)
        for k in range(3):
            new = mid[k] + w0[3 + k, 8 * q : 8 * q + 8] * res[k]
            out[k, 8 * q - 8 : 8 * q, :] = new[:, own_cols]

    for dr, dc in ways:
        @when(rowhas[dr], has[dc])
        def _(dr=dr, dc=dc):
            halo(dr, dc).wait_send()
    for dt, dc in partners:
        @when(has[dc])
        def _(dt=dt, dc=dc):
            gather(coef_slots, coef_send, coef_recv, dt, dc).wait_send()
            gather(src_slots, src_send, src_recv, dt, dc).wait_send()


def on_device(right_side, noise_block, edges):
    T, NB, NS = lax.axis_size("tiles"), lax.axis_size("band"), lax.axis_size("stokes")
    _, h, w = right_side.shape
    shapes = [
        (h + 2 * HALO, w + SIDE),
        (h // 2 + 16, w // 2 + SIDE),
        (h // 4 * T, 3 * SIDE),
        (max(8, h // 8 * T), 2 * SIDE),
        (max(8, h // 16 * T), SIDE),
    ]
    scratch = []
    for i, (n, m) in enumerate(shapes):
        scratch += [
            pltpu.VMEM((11, n, m), F32),
            pltpu.VMEM((3, n + 16, m), F32),
            pltpu.VMEM((3, n + 16, m), F32),
            pltpu.VMEM((6, n, m), F32),
        ]
        if i < 4:
            scratch.append(pltpu.VMEM((3 * n, m), F32))
    scratch += [
        pltpu.VMEM((6, max(8 * 32, 6 * h // 4 * T), SIDE), F32),
        pltpu.VMEM((48, 3 * SIDE), F32),
        pltpu.VMEM((2, h, SIDE), F32),
        pltpu.VMEM((2, h + 2 * HALO, SIDE), F32),
        pltpu.VMEM((T, 3, 32, SIDE), F32),
        pltpu.VMEM((T, 3, 16, SIDE), F32),
        pltpu.VMEM((2, 3, 8, 3 * SIDE), F32),
        pltpu.SemaphoreType.DMA((3,)),
        pltpu.SemaphoreType.DMA((9,)),
        pltpu.SemaphoreType.DMA((9,)),
        pltpu.SemaphoreType.DMA((T, 3)),
        pltpu.SemaphoreType.DMA((T, 3)),
        pltpu.SemaphoreType.DMA((T, 3)),
        pltpu.SemaphoreType.DMA((T, 3)),
        pltpu.SemaphoreType.DMA((2,)),
        pltpu.SemaphoreType.DMA((2,)),
    ]
    return pl.pallas_call(
        functools.partial(kernel, T, NB, NS),
        out_shape=jax.ShapeDtypeStruct(right_side.shape, F32),
        in_specs=[pl.BlockSpec(memory_space=pltpu.HBM)] * 3,
        out_specs=pl.BlockSpec(memory_space=pltpu.VMEM),
        scratch_shapes=scratch,
        compiler_params=pltpu.CompilerParams(
            collective_id=0, has_side_effects=True, vmem_limit_bytes=60 * 1024 * 1024
        ),
    )(right_side, noise_block, edges)


def solution(mesh):
    spec = P(None, ("groups", "tiles"), ("band", "stokes"))
    return jax.shard_map(
        on_device, mesh=mesh, in_specs=(spec, spec, spec), out_specs=spec, check_vma=False
    )
```

```python
import functools

import jax
import jax.numpy as jnp
from jax import lax
from jax.experimental import pallas as pl
from jax.experimental.pallas import tpu as pltpu
from jax.sharding import PartitionSpec as P

OMEGA = 0.8
COARSE_SWEEPS = 8
HALO = 8
SIDE = 128
DEEP = 11
NEAR_ROWS = (6, 6, 6, 6, 6, 6, 5, 5, 5, 7, 6)
MESH = pl.DeviceIdType.MESH
F32 = jnp.float32


def rounded(x):
    return x.astype(jnp.bfloat16).astype(F32)


def dot(x, y):
    n = x.shape[0]
    high = rounded(x)
    rest = x - high
    mid = rounded(rest)
    pieces = jnp.concatenate([high, mid, rest - mid], 0)
    z = jnp.dot(pieces, y, precision=lax.Precision.DEFAULT, preferred_element_type=F32)
    return z[:n] + (z[n : 2 * n] + z[2 * n :])


def iota(shape, dim):
    return lax.broadcasted_iota(jnp.int32, shape, dim)


def ones(hit):
    return jnp.where(hit, 1.0, 0.0).astype(F32)


def half(i):
    return lax.shift_right_logical(i, 1)


def pool_matrix(n, m, odd=False):
    c, j = iota((n, m), 0), iota((n, m), 1)
    hit = c == 2 * j + 1
    return ones(hit if odd else hit | (c == 2 * j))


def spread_matrix(n, m):
    c, j = iota((n, m), 0), iota((n, m), 1)
    return ones(c == half(j))


def ring_pool(cut, odd=False):
    c, j = iota((SIDE, SIDE), 0), iota((SIDE, SIDE), 1)
    hit = j == half(c) + jnp.where(c >= cut, 64, 0)
    return ones(hit & ((c & 1) == 1) if odd else hit)


def ring_spread(n, m, cut):
    c, j = iota((n, m), 0), iota((n, m), 1)
    return ones(c == half(j) + jnp.where(j >= cut, 64, 0))


def chunks(a):
    return range(a.shape[1] // 8)


def setup(a, aux):
    for q in chunks(a):
        rows = slice(8 * q, 8 * q + 8)
        down, right = a[9, rows], a[10, rows]
        if q == 0:
            up = jnp.where(iota(down.shape, 0) == 0, 0.0, pltpu.roll(down, 1, 0))
        else:
            up = a[9, 8 * q - 1 : 8 * q + 7]
        left = pltpu.roll(right, 1, 1)
        total = down + up + right + left
        aux[0, rows], aux[1, rows], aux[2, rows] = up, left, total
        for k in range(3):
            aux[3 + k, rows] = jnp.where(down > 0, OMEGA / (a[3 + k, rows] + total), 0.0)


def first(a, aux, v):
    for q in chunks(a):
        rows = slice(8 * q, 8 * q + 8)
        for k in range(3):
            v[k, 8 + 8 * q : 16 + 8 * q] = aux[3 + k, rows] * a[k, rows]


def residual_at(a, aux, v, q):
    rows = slice(8 * q, 8 * q + 8)
    mid = [v[k, 8 + 8 * q : 16 + 8 * q] for k in range(3)]
    n = [a[3 + i, rows] for i in range(6)]
    down, right, up, left, total = a[9, rows], a[10, rows], aux[0, rows], aux[1, rows], aux[2, rows]
    width = mid[0].shape[1]
    image = [
        n[0] * mid[0] + n[3] * mid[1] + n[4] * mid[2],
        n[3] * mid[0] + n[1] * mid[1] + n[5] * mid[2],
        n[4] * mid[0] + n[5] * mid[1] + n[2] * mid[2],
    ]
    out = []
    for k in range(3):
        near = (
            down * v[k, 9 + 8 * q : 17 + 8 * q]
            + up * v[k, 7 + 8 * q : 15 + 8 * q]
            + right * pltpu.roll(mid[k], width - 1, 1)
            + left * pltpu.roll(mid[k], 1, 1)
        )
        out.append(a[k, rows] - (image[k] + total * mid[k] - near))
    return mid, out


def sweep(a, aux, src, dst, which=None):
    for q in chunks(a) if which is None else which:
        mid, res = residual_at(a, aux, src, q)
        for k in range(3):
            dst[k, 8 + 8 * q : 16 + 8 * q] = mid[k] + aux[3 + k, 8 * q : 8 * q + 8] * res[k]


def residual(a, aux, v, r):
    height = a.shape[1]
    for q in chunks(a):
        _, res = residual_at(a, aux, v, q)
        for k in range(3):
            r[k * height + 8 * q : k * height + 8 * q + 8, :] = res[k]


def pool_lanes(x, matrix, tail=None):
    n = matrix.shape[0]
    width = x.shape[1]
    parts = []
    for b in range(0, width, n):
        if b + n <= width:
            parts.append(dot(x[:, b : b + n], matrix))
        else:
            parts.append(dot(x[:, b:width], matrix[: width - b] if tail is None else tail))
    return parts


def pool_rows(parts, st, odd=False):
    out = []
    for b, part in enumerate(parts):
        n = part.shape[0]
        st[b, 0:n, :] = part
        top = st[b, pl.ds(1, n // 2, stride=2), :]
        out.append(top if odd else top + st[b, pl.ds(0, n // 2, stride=2), :])
    return out


def coarsen_coefficients(arrays, st, even, odd):
    h = arrays[0].shape[0]
    parts = pool_lanes(jnp.concatenate(arrays[:7], 0), even)
    noise = pool_rows([p[: 6 * h] for p in parts], st)
    down = pool_rows([p[6 * h :] for p in parts], st, odd=True)
    right = pool_rows(pool_lanes(arrays[7], odd), st)
    h = h // 2
    out = []
    for i in range(6):
        out.append([p[i * h : i * h + h] for p in noise])
    return out + [down, right]


def spread_rows(parts, st):
    for b, part in enumerate(parts):
        n = part.shape[0]
        st[b, pl.ds(0, n, stride=2), :] = part
        st[b, pl.ds(1, n, stride=2), :] = part


def put(a, channel, row, parts, tile=0):
    for b, part in enumerate(parts, tile):
        a[channel, row : row + part.shape[0], SIDE * b : SIDE * b + SIDE] = part


def add_spread(v, dst, st, stride, blocks, height, row0=0):
    for k in range(3):
        for b in range(blocks):
            lanes = slice(SIDE * b, SIDE * b + SIDE)
            dst[k, 8 : 8 + height, lanes] = v[k, 8 : 8 + height, lanes] + st[b, stride * k + row0 : stride * k + row0 + height, :]


def kernel(
    T, NB, NS, rhs, noise, edges, out,
    a0, x0, u0, w0, r0, a1, x1, u1, w1, r1, a2, x2, u2, w2, r2, a3, x3, u3, w3, r3, a4, x4, u4, w4,
    st, win, sent, got, rows_sent, rows_got,
    coef_own, coef_side, coef_pack, src_own, src_side, src_pack, side_rows,
    in_sem, halo_send, halo_recv, coef_send, coef_recv, src_send, src_recv, row_send, row_recv,
):
    t = lax.axis_index("tiles")
    col = lax.axis_index("band") * NS + lax.axis_index("stokes")
    cols = NB * NS
    h, w = rhs.shape[1], rhs.shape[2]
    has = {-1: col > 0, 0: None, 1: col < cols - 1}
    rowhas = {-1: t > 0, 0: None, 1: t < T - 1}

    def when(*conds):
        conds = [c for c in conds if c is not None]
        if not conds:
            return lambda f: f()
        return pl.when(functools.reduce(jnp.logical_and, conds))

    def device(tile, dc):
        c = col + dc
        return {"tiles": tile, "band": c // NS, "stokes": lax.rem(c, NS)}

    own_rows, own_cols = slice(HALO, HALO + h), slice(0, w)
    loads = [
        pltpu.make_async_copy(rhs, a0.at[0:3, own_rows, own_cols], in_sem.at[0]),
        pltpu.make_async_copy(noise, a0.at[3:9, own_rows, own_cols], in_sem.at[1]),
        pltpu.make_async_copy(edges, a0.at[9:11, own_rows, own_cols], in_sem.at[2]),
    ]
    for c in loads:
        c.start()

    partners = [(dt, dc) for dc in (-1, 0, 1) for dt in range(T) if dt or dc]
    barrier = pltpu.get_barrier_semaphore()
    for dt, dc in partners:
        @when(has[dc])
        def _(dt=dt, dc=dc):
            pl.semaphore_signal(barrier, inc=1, device_id=device(lax.rem(t + dt, T), dc), device_id_type=MESH)

    @pl.when(t == 0)
    def _():
        got[:, 0:HALO] = jnp.zeros_like(got[:, 0:HALO])
        side_rows[0] = jnp.zeros_like(side_rows[0])

    @pl.when(t == T - 1)
    def _():
        got[:, HALO + h :] = jnp.zeros_like(got[:, HALO + h :])
        side_rows[1] = jnp.zeros_like(side_rows[1])

    @pl.when(col == 0)
    def _():
        got[0] = jnp.zeros_like(got[0])
        coef_side[:, 0] = jnp.zeros_like(coef_side[:, 0])
        src_side[:, 0] = jnp.zeros_like(src_side[:, 0])

    @pl.when(col == cols - 1)
    def _():
        got[1] = jnp.zeros_like(got[1])
        coef_side[:, 1] = jnp.zeros_like(coef_side[:, 1])
        src_side[:, 1] = jnp.zeros_like(src_side[:, 1])

    a0[:, 0:HALO, own_cols] = jnp.zeros_like(a0[:, 0:HALO, own_cols])
    a0[:, HALO + h :, own_cols] = jnp.zeros_like(a0[:, HALO + h :, own_cols])
    for a in (a1, a3, a4):
        a[...] = jnp.zeros_like(a)
    for v in (x0, u0, x1, u1, x2, u2, x3, u3, x4, u4):
        v[:, 0:8, :] = jnp.zeros_like(v[:, 0:8, :])
        n = v.shape[1]
        v[:, n - 8 : n, :] = jnp.zeros_like(v[:, n - 8 : n, :])

    for c in loads:
        c.wait()

    lane = iota((8, SIDE), 1)
    for q in range(h // 8):
        rows = slice(HALO + 8 * q, HALO + 8 * q + 8)
        head = tail = jnp.zeros((8, SIDE), F32)
        for i in range(11):
            here = (lane >= DEEP * i) & (lane < DEEP * i + DEEP)
            one, two = a0[i, rows, 0:SIDE], a0[i, rows, w - SIDE : w]
            head = jnp.where(here, pltpu.roll(one, DEEP * i, 1) if i else one, head)
            tail = jnp.where(here, pltpu.roll(two, (DEEP * i + DEEP) % SIDE, 1), tail)
        sent[0, 8 * q : 8 * q + 8], sent[1, 8 * q : 8 * q + 8] = head, tail
    at = 0
    for i, n in enumerate(NEAR_ROWS):
        rows_sent[0, at : at + n] = a0[i, HALO : HALO + n, own_cols]
        rows_sent[1, at : at + n] = a0[i, HALO + h - n : HALO + h, own_cols]
        at += n

    sides = 1 + jnp.where(col > 0, 1, 0) + jnp.where(col < cols - 1, 1, 0)
    pl.semaphore_wait(barrier, sides * T - 1)

    row_dst = {-1: slice(HALO + h, 2 * HALO + h), 0: own_rows, 1: slice(0, HALO)}
    part_src = {-1: slice(0, HALO), 0: slice(0, h), 1: slice(h - HALO, h)}

    def halo(dr, dc):
        i = (dr + 1) * 3 + dc + 1
        if dc:
            src = sent.at[(dc + 1) // 2, part_src[dr]]
            dst = got.at[(1 - dc) // 2, row_dst[dr]]
        else:
            src, dst = rows_sent.at[(dr + 1) // 2], rows_got.at[(1 - dr) // 2]
        return pltpu.make_async_remote_copy(
            src_ref=src,
            dst_ref=dst,
            send_sem=halo_send.at[i],
            recv_sem=halo_recv.at[i],
            device_id=device(t + dr, dc),
            device_id_type=MESH,
        )

    ways = [(0, -1), (0, 1), (-1, -1), (-1, 1), (1, -1), (1, 1), (-1, 0), (1, 0)]
    for dr, dc in ways:
        @when(rowhas[dr], has[dc])
        def _(dr=dr, dc=dc):
            halo(dr, dc).start()

    def gather(own, side, pack, send, recv, dt, dc):
        if dc:
            src, dst = pack.at[(dc + 1) // 2], side.at[t, (1 - dc) // 2]
        else:
            src, dst = own.at[t], own.at[t]
        return pltpu.make_async_remote_copy(
            src_ref=src,
            dst_ref=dst,
            send_sem=send.at[dt, dc + 1],
            recv_sem=recv.at[t, 1 - dc],
            device_id=device(lax.rem(t + dt, T), dc),
            device_id_type=MESH,
        )

    def arrival(own, side, pack, send, recv, dt, dc):
        s = lax.rem(t + dt, T)
        dst = side.at[s, (dc + 1) // 2] if dc else own.at[s]
        return pltpu.make_async_remote_copy(
            src_ref=dst,
            dst_ref=dst,
            send_sem=send.at[dt, dc + 1],
            recv_sem=recv.at[s, dc + 1],
            device_id=device(s, dc),
            device_id_type=MESH,
        )

    coef = (coef_own, coef_side, coef_pack, coef_send, coef_recv)
    src = (src_own, src_side, src_pack, src_send, src_recv)

    def scatter(x, way):
        own, pack = way[0], way[2]
        n = x.shape[0] // 2
        low = iota((n, SIDE), 1) < 64
        own[t] = x
        pack[0] = jnp.where(low, x[:n], pltpu.roll(x[n:], 64, 1))
        pack[1] = jnp.where(low, pltpu.roll(x[:n], 64, 1), x[n:])
        for dt, dc in partners:
            @when(has[dc])
            def _(dt=dt, dc=dc):
                gather(*way, dt, dc).start()

    def assemble(way, channel, count):
        for dt, dc in partners:
            @when(has[dc])
            def _(dt=dt, dc=dc):
                arrival(*way, dt, dc).wait_recv()
        own, side = way[:2]
        n = side.shape[2]
        low = iota((n, SIDE), 1) < 64

        def beside(s):
            left, right = side[s, 0], side[s, 1]
            return jnp.concatenate(
                [jnp.where(low, right, pltpu.roll(left, 64, 1)), jnp.where(low, pltpu.roll(right, 64, 1), left)], 0
            )

        for j in range(T // 2):
            for c in range(2):
                one, two = (beside(2 * j), beside(2 * j + 1)) if c else (own[2 * j], own[2 * j + 1])
                for i in range(count):
                    a2[channel + i, 8 * j : 8 * j + 8, SIDE * c : SIDE * c + SIDE] = jnp.concatenate(
                        [one[4 * i : 4 * i + 4], two[4 * i : 4 * i + 4]], 0
                    )

    even, odd = pool_matrix(256, 128), pool_matrix(256, 128, odd=True)
    even_ring, odd_ring = ring_pool(64), ring_pool(64, odd=True)
    wide = spread_matrix(128, 256)

    fine = [a0[3 + i, own_rows, own_cols] for i in range(8)]
    mid = coarsen_coefficients(fine, st, even, odd)
    for i in range(8):
        put(a1, 3 + i, 8, mid[i])
    mid = [jnp.concatenate(parts, 1) for parts in mid]
    low = [parts[0] for parts in coarsen_coefficients(mid, st, even, odd)]
    scatter(jnp.concatenate(low, 0), coef)

    for dr, dc in ways:
        if dc:
            @when(rowhas[dr], has[dc])
            def _(dr=dr, dc=dc):
                halo(-dr, -dc).wait_recv()

    for q in range(a0.shape[1] // 8):
        rows = slice(8 * q, 8 * q + 8)
        for i in range(11):
            right = pltpu.roll(got[1, rows], SIDE - DEEP * i, 1) if i else got[1, rows]
            left = pltpu.roll(got[0, rows], SIDE - DEEP - DEEP * i, 1)
            a0[i, rows, w : w + SIDE] = jnp.where(
                lane < DEEP, right, jnp.where(lane >= SIDE - DEEP, left, 0.0)
            )

    ends = [a0[3 + i, :, w : w + SIDE] for i in range(8)]
    for i, parts in enumerate(coarsen_coefficients(ends, st, even_ring, odd_ring)):
        put(a1, 3 + i, 4, parts, 2)

    for dr in (-1, 1):
        @when(rowhas[dr])
        def _(dr=dr):
            halo(-dr, 0).wait_recv()
            at = 0
            for i, n in enumerate(NEAR_ROWS):
                top = HALO - n if dr < 0 else HALO + h
                a0[i, top : top + n, own_cols] = rows_got[(dr + 1) // 2, at : at + n]
                at += n

    setup(a0, w0)
    first(a0, w0, x0)
    sweep(a0, w0, x0, u0)
    residual(a0, w0, u0, r0)
    source = pool_rows(pool_lanes(r0[...], even, even_ring), st)
    h1 = a0.shape[1] // 2
    for k in range(3):
        put(a1, k, 4, [p[k * h1 : k * h1 + h1] for p in source])
    beside = [
        jnp.concatenate([a0[3 + i, 0:HALO, own_cols], a0[3 + i, HALO + h :, own_cols]], 0) for i in range(8)
    ]
    for i, parts in enumerate(coarsen_coefficients(beside, st, even, odd)):
        put(a1, 3 + i, 4, [p[:4] for p in parts])
        put(a1, 3 + i, 16, [p[4:] for p in parts])
    setup(a1, w1)
    first(a1, w1, x1)
    sweep(a1, w1, x1, u1)
    residual(a1, w1, u1, r1)
    own = dot(r1[:, 0:256], even)
    source = pool_rows([own], st)[0]
    packed = [source[12 * k + 4 : 12 * k + 8] for k in range(3)]
    scatter(jnp.concatenate(packed + [jnp.zeros((4, SIDE), F32)], 0), src)

    def rows_copy(dr):
        i = (dr + 1) // 2
        return pltpu.make_async_remote_copy(
            src_ref=u1.at[:, 16:24, :],
            dst_ref=side_rows.at[1 - i],
            send_sem=row_send.at[i],
            recv_sem=row_recv.at[1 - i],
            device_id=device(t + dr, 0),
            device_id_type=MESH,
        )

    for dr in (-1, 1):
        @when(rowhas[dr])
        def _(dr=dr):
            rows_copy(dr).start()

    assemble(coef, 3, 8)
    setup(a2, w2)
    last, last_odd = ring_pool(96), ring_pool(96, odd=True)
    for a, b, aux, p, p_odd in ((a2, a3, w3, even, odd), (a3, a4, w4, last, last_odd)):
        for i, parts in enumerate(coarsen_coefficients([a[3 + i] for i in range(8)], st, p, p_odd)):
            put(b, 3 + i, 0, parts)
        setup(b, aux)
    assemble(src, 0, 3)

    for a, aux, x, u, r, b, p in ((a2, w2, x2, u2, r2, a3, even), (a3, w3, x3, u3, r3, a4, last)):
        first(a, aux, x)
        sweep(a, aux, x, u)
        residual(a, aux, u, r)
        source = pool_rows(pool_lanes(r[...], p), st)
        n = a.shape[1] // 2
        for k in range(3):
            put(b, k, 0, [z[k * n : k * n + n] for z in source])
    first(a4, w4, x4)
    now, then = x4, u4
    for _ in range(COARSE_SWEEPS - 1):
        sweep(a4, w4, now, then)
        now, then = then, now
    coarse = now
    for a, aux, x, u in ((a3, w3, x3, u3), (a2, w2, x2, u2)):
        n = coarse.shape[1] - 16
        y = jnp.concatenate([coarse[k, 8 : 8 + n] for k in range(3)], 0)
        z = dot(y, wide if a is a2 else ring_spread(SIDE, SIDE, 96))
        parts = [z[:, b : b + SIDE] for b in range(0, z.shape[1], SIDE)]
        spread_rows(parts, st)
        add_spread(u, x, st, 2 * n, len(parts), a.shape[1])
        sweep(a, aux, x, u)
        sweep(a, aux, u, x)
        coarse = x

    for s in range(T):
        @pl.when(t == s)
        def _(s=s):
            for k in range(3):
                win[16 * k : 16 * k + 16, :] = x2[k, 4 + 4 * s : 20 + 4 * s]
    y = dot(win[...], ring_spread(256, 384, 320))
    spread_rows([y[:, 128 * b : 128 * b + 128] for b in range(3)], st)
    for dr in (-1, 1):
        @when(rowhas[dr])
        def _(dr=dr):
            rows_copy(dr).wait_send()
            rows_copy(-dr).wait_recv()
    u1[:, 8:16, :] = side_rows[0]
    u1[:, 24:32, :] = side_rows[1]
    add_spread(u1, x1, st, 32, 3, 24)
    sweep(a1, w1, x1, u1)
    sweep(a1, w1, u1, x1)

    y = jnp.concatenate([x1[k, 8:32] for k in range(3)], 0)
    parts = []
    for b in range(2):
        z = dot(y[:, 128 * b : 128 * b + 128], wide)
        parts += [z[:, :128], z[:, 128:]]
    parts.append(dot(y[:, 256:384], ring_spread(SIDE, SIDE, 64)))
    spread_rows(parts, st)
    add_spread(u0, x0, st, 48, 5, 32, row0=8)
    sweep(a0, w0, x0, u0)
    for q in range(1, 1 + h // 8):
        mid, res = residual_at(a0, w0, u0, q)
        for k in range(3):
            new = mid[k] + w0[3 + k, 8 * q : 8 * q + 8] * res[k]
            out[k, 8 * q - 8 : 8 * q, :] = new[:, own_cols]

    for dr, dc in ways:
        @when(rowhas[dr], has[dc])
        def _(dr=dr, dc=dc):
            halo(dr, dc).wait_send()
    for dt, dc in partners:
        @when(has[dc])
        def _(dt=dt, dc=dc):
            gather(*coef, dt, dc).wait_send()
            gather(*src, dt, dc).wait_send()


def on_device(right_side, noise_block, edges):
    T, NB, NS = lax.axis_size("tiles"), lax.axis_size("band"), lax.axis_size("stokes")
    _, h, w = right_side.shape
    shapes = [
        (h + 2 * HALO, w + SIDE),
        (h // 2 + 16, w // 2 + SIDE),
        (h // 4 * T, 2 * SIDE),
        (max(8, h // 8 * T), SIDE),
        (max(8, h // 16 * T), SIDE),
    ]
    scratch = []
    for i, (n, m) in enumerate(shapes):
        scratch += [
            pltpu.VMEM((11, n, m), F32),
            pltpu.VMEM((3, n + 16, m), F32),
            pltpu.VMEM((3, n + 16, m), F32),
            pltpu.VMEM((6, n, m), F32),
        ]
        if i < 4:
            scratch.append(pltpu.VMEM((3 * n, m), F32))
    scratch += [
        pltpu.VMEM((6, max(8 * 32, 6 * h // 4 * T), SIDE), F32),
        pltpu.VMEM((48, 2 * SIDE), F32),
        pltpu.VMEM((2, h, SIDE), F32),
        pltpu.VMEM((2, h + 2 * HALO, SIDE), F32),
        pltpu.VMEM((2, sum(NEAR_ROWS), w), F32),
        pltpu.VMEM((2, sum(NEAR_ROWS), w), F32),
        pltpu.VMEM((T, 32, SIDE), F32),
        pltpu.VMEM((T, 2, 16, SIDE), F32),
        pltpu.VMEM((2, 16, SIDE), F32),
        pltpu.VMEM((T, 16, SIDE), F32),
        pltpu.VMEM((T, 2, 8, SIDE), F32),
        pltpu.VMEM((2, 8, SIDE), F32),
        pltpu.VMEM((2, 3, 8, 3 * SIDE), F32),
        pltpu.SemaphoreType.DMA((3,)),
        pltpu.SemaphoreType.DMA((9,)),
        pltpu.SemaphoreType.DMA((9,)),
        pltpu.SemaphoreType.DMA((T, 3)),
        pltpu.SemaphoreType.DMA((T, 3)),
        pltpu.SemaphoreType.DMA((T, 3)),
        pltpu.SemaphoreType.DMA((T, 3)),
        pltpu.SemaphoreType.DMA((2,)),
        pltpu.SemaphoreType.DMA((2,)),
    ]
    return pl.pallas_call(
        functools.partial(kernel, T, NB, NS),
        out_shape=jax.ShapeDtypeStruct(right_side.shape, F32),
        in_specs=[pl.BlockSpec(memory_space=pltpu.HBM)] * 3,
        out_specs=pl.BlockSpec(memory_space=pltpu.VMEM),
        scratch_shapes=scratch,
        compiler_params=pltpu.CompilerParams(
            collective_id=0, has_side_effects=True, vmem_limit_bytes=60 * 1024 * 1024
        ),
    )(right_side, noise_block, edges)


def solution(mesh):
    spec = P(None, ("groups", "tiles"), ("band", "stokes"))
    return jax.shard_map(
        on_device, mesh=mesh, in_specs=(spec, spec, spec), out_specs=spec, check_vma=False
    )
```

```python
import functools
import itertools

import jax
import jax.numpy as jnp
from jax import lax
from jax.experimental import pallas as pl
from jax.experimental.pallas import tpu as pltpu
from jax.sharding import PartitionSpec as P

OMEGA = 0.8
COARSE_SWEEPS = 8
HALO = 8
SIDE = 128
DEEP = 11
BUFFERS = 12
NEAR_ROWS = (6, 6, 6, 6, 6, 6, 5, 5, 5, 7, 6)
MESH = pl.DeviceIdType.MESH
F32 = jnp.float32


def rounded(x):
    return x.astype(jnp.bfloat16).astype(F32)


def dot(x, y):
    n = x.shape[0]
    high = rounded(x)
    rest = x - high
    mid = rounded(rest)
    pieces = jnp.concatenate([high, mid, rest - mid], 0)
    z = jnp.dot(pieces, y, precision=lax.Precision.DEFAULT, preferred_element_type=F32)
    return z[:n] + (z[n : 2 * n] + z[2 * n :])


def iota(shape, dim):
    return lax.broadcasted_iota(jnp.int32, shape, dim)


def ones(hit):
    return jnp.where(hit, 1.0, 0.0).astype(F32)


def half(i):
    return lax.shift_right_logical(i, 1)


def pool_matrix(n, m, odd=False):
    c, j = iota((n, m), 0), iota((n, m), 1)
    hit = c == 2 * j + 1
    return ones(hit if odd else hit | (c == 2 * j))


def spread_matrix(n, m):
    c, j = iota((n, m), 0), iota((n, m), 1)
    return ones(c == half(j))


def ring_pool(cut, odd=False):
    c, j = iota((SIDE, SIDE), 0), iota((SIDE, SIDE), 1)
    hit = j == half(c) + jnp.where(c >= cut, 64, 0)
    return ones(hit & ((c & 1) == 1) if odd else hit)


def ring_spread(n, m, cut):
    c, j = iota((n, m), 0), iota((n, m), 1)
    return ones(c == half(j) + jnp.where(j >= cut, 64, 0))


def chunks(a):
    return range(a.shape[1] // 8)


def setup(a, aux):
    for q in chunks(a):
        rows = slice(8 * q, 8 * q + 8)
        down, right = a[9, rows], a[10, rows]
        if q == 0:
            up = jnp.where(iota(down.shape, 0) == 0, 0.0, pltpu.roll(down, 1, 0))
        else:
            up = a[9, 8 * q - 1 : 8 * q + 7]
        left = pltpu.roll(right, 1, 1)
        total = down + up + right + left
        aux[0, rows], aux[1, rows], aux[2, rows] = up, left, total
        for k in range(3):
            aux[3 + k, rows] = jnp.where(down > 0, OMEGA / (a[3 + k, rows] + total), 0.0)


def first(a, aux, v):
    for q in chunks(a):
        rows = slice(8 * q, 8 * q + 8)
        for k in range(3):
            v[k, 8 + 8 * q : 16 + 8 * q] = aux[3 + k, rows] * a[k, rows]


def residual_at(a, aux, v, q):
    rows = slice(8 * q, 8 * q + 8)
    mid = [v[k, 8 + 8 * q : 16 + 8 * q] for k in range(3)]
    n = [a[3 + i, rows] for i in range(6)]
    down, right, up, left, total = a[9, rows], a[10, rows], aux[0, rows], aux[1, rows], aux[2, rows]
    width = mid[0].shape[1]
    image = [
        n[0] * mid[0] + n[3] * mid[1] + n[4] * mid[2],
        n[3] * mid[0] + n[1] * mid[1] + n[5] * mid[2],
        n[4] * mid[0] + n[5] * mid[1] + n[2] * mid[2],
    ]
    out = []
    for k in range(3):
        near = (
            down * v[k, 9 + 8 * q : 17 + 8 * q]
            + up * v[k, 7 + 8 * q : 15 + 8 * q]
            + right * pltpu.roll(mid[k], width - 1, 1)
            + left * pltpu.roll(mid[k], 1, 1)
        )
        out.append(a[k, rows] - (image[k] + total * mid[k] - near))
    return mid, out


def sweep(a, aux, src, dst, which=None):
    for q in chunks(a) if which is None else which:
        mid, res = residual_at(a, aux, src, q)
        for k in range(3):
            dst[k, 8 + 8 * q : 16 + 8 * q] = mid[k] + aux[3 + k, 8 * q : 8 * q + 8] * res[k]


def residual(a, aux, v, r):
    height = a.shape[1]
    for q in chunks(a):
        _, res = residual_at(a, aux, v, q)
        for k in range(3):
            r[k * height + 8 * q : k * height + 8 * q + 8, :] = res[k]


def pool_lanes(x, matrix, tail=None):
    n = matrix.shape[0]
    width = x.shape[1]
    parts = []
    for b in range(0, width, n):
        if b + n <= width:
            parts.append(dot(x[:, b : b + n], matrix))
        else:
            parts.append(dot(x[:, b:width], matrix[: width - b] if tail is None else tail))
    return parts


def pool_rows(parts, st, odd=False):
    st = st()
    out = []
    for b, part in enumerate(parts):
        n = part.shape[0]
        st[b, 0:n, :] = part
        top = st[b, pl.ds(1, n // 2, stride=2), :]
        out.append(top if odd else top + st[b, pl.ds(0, n // 2, stride=2), :])
    return out


def coarsen_coefficients(arrays, st, even, odd):
    h = arrays[0].shape[0]
    parts = pool_lanes(jnp.concatenate(arrays[:7], 0), even)
    noise = pool_rows([p[: 6 * h] for p in parts], st)
    down = pool_rows([p[6 * h :] for p in parts], st, odd=True)
    right = pool_rows(pool_lanes(arrays[7], odd), st)
    h = h // 2
    out = []
    for i in range(6):
        out.append([p[i * h : i * h + h] for p in noise])
    return out + [down, right]


def spread_rows(parts, st):
    st = st()
    for b, part in enumerate(parts):
        n = part.shape[0]
        st[b, pl.ds(0, n, stride=2), :] = part
        st[b, pl.ds(1, n, stride=2), :] = part
    return st


def put(a, channel, row, parts, tile=0):
    for b, part in enumerate(parts, tile):
        a[channel, row : row + part.shape[0], SIDE * b : SIDE * b + SIDE] = part


def add_spread(v, dst, st, stride, blocks, height, row0=0):
    for k in range(3):
        for b in range(blocks):
            lanes = slice(SIDE * b, SIDE * b + SIDE)
            dst[k, 8 : 8 + height, lanes] = v[k, 8 : 8 + height, lanes] + st[b, stride * k + row0 : stride * k + row0 + height, :]


def kernel(
    T, NB, NS, stack, out,
    a0, x0, u0, w0, r0, a1, x1, u1, w1, r1, a2, x2, u2, w2, r2, a3, x3, u3, w3, r3, a4, x4, u4, w4,
    tiles, win, sent, got, rows_sent, rows_got,
    coef_own, coef_side, coef_pack, src_own, src_side, src_pack, side_rows,
    in_sem, halo_send, halo_recv, coef_send, coef_recv, src_send, src_recv, row_send, row_recv,
):
    turn = itertools.cycle(range(BUFFERS))

    def st():
        return tiles.at[next(turn)]

    t = lax.axis_index("tiles")
    col = lax.axis_index("band") * NS + lax.axis_index("stokes")
    cols = NB * NS
    h, w = stack.shape[1], stack.shape[2]
    has = {-1: col > 0, 0: None, 1: col < cols - 1}
    rowhas = {-1: t > 0, 0: None, 1: t < T - 1}

    def when(*conds):
        conds = [c for c in conds if c is not None]
        if not conds:
            return lambda f: f()
        return pl.when(functools.reduce(jnp.logical_and, conds))

    def device(tile, dc):
        c = col + dc
        return {"tiles": tile, "band": c // NS, "stokes": lax.rem(c, NS)}

    own_rows, own_cols = slice(HALO, HALO + h), slice(0, w)
    load = pltpu.make_async_copy(stack, a0.at[:, own_rows, own_cols], in_sem.at[0])
    load.start()

    partners = [(dt, dc) for dc in (-1, 0, 1) for dt in range(T) if dt or dc]
    barrier = pltpu.get_barrier_semaphore()
    for dt, dc in partners:
        @when(has[dc])
        def _(dt=dt, dc=dc):
            pl.semaphore_signal(barrier, inc=1, device_id=device(lax.rem(t + dt, T), dc), device_id_type=MESH)

    @pl.when(t == 0)
    def _():
        got[:, 0:HALO] = jnp.zeros_like(got[:, 0:HALO])
        side_rows[0] = jnp.zeros_like(side_rows[0])

    @pl.when(t == T - 1)
    def _():
        got[:, HALO + h :] = jnp.zeros_like(got[:, HALO + h :])
        side_rows[1] = jnp.zeros_like(side_rows[1])

    @pl.when(col == 0)
    def _():
        got[0] = jnp.zeros_like(got[0])
        coef_side[:, 0] = jnp.zeros_like(coef_side[:, 0])
        src_side[:, 0] = jnp.zeros_like(src_side[:, 0])

    @pl.when(col == cols - 1)
    def _():
        got[1] = jnp.zeros_like(got[1])
        coef_side[:, 1] = jnp.zeros_like(coef_side[:, 1])
        src_side[:, 1] = jnp.zeros_like(src_side[:, 1])

    a0[:, 0:HALO, own_cols] = jnp.zeros_like(a0[:, 0:HALO, own_cols])
    a0[:, HALO + h :, own_cols] = jnp.zeros_like(a0[:, HALO + h :, own_cols])
    for a in (a1, a3, a4):
        a[...] = jnp.zeros_like(a)
    for v in (x0, u0, x1, u1, x2, u2, x3, u3, x4, u4):
        v[:, 0:8, :] = jnp.zeros_like(v[:, 0:8, :])
        n = v.shape[1]
        v[:, n - 8 : n, :] = jnp.zeros_like(v[:, n - 8 : n, :])

    load.wait()

    lane = iota((8, SIDE), 1)
    for q in range(h // 8):
        rows = slice(HALO + 8 * q, HALO + 8 * q + 8)
        head = tail = jnp.zeros((8, SIDE), F32)
        for i in range(11):
            here = (lane >= DEEP * i) & (lane < DEEP * i + DEEP)
            one, two = a0[i, rows, 0:SIDE], a0[i, rows, w - SIDE : w]
            head = jnp.where(here, pltpu.roll(one, DEEP * i, 1) if i else one, head)
            tail = jnp.where(here, pltpu.roll(two, (DEEP * i + DEEP) % SIDE, 1), tail)
        sent[0, 8 * q : 8 * q + 8], sent[1, 8 * q : 8 * q + 8] = head, tail
    at = 0
    for i, n in enumerate(NEAR_ROWS):
        rows_sent[0, at : at + n] = a0[i, HALO : HALO + n, own_cols]
        rows_sent[1, at : at + n] = a0[i, HALO + h - n : HALO + h, own_cols]
        at += n

    sides = 1 + jnp.where(col > 0, 1, 0) + jnp.where(col < cols - 1, 1, 0)
    pl.semaphore_wait(barrier, sides * T - 1)

    row_dst = {-1: slice(HALO + h, 2 * HALO + h), 0: own_rows, 1: slice(0, HALO)}
    part_src = {-1: slice(0, HALO), 0: slice(0, h), 1: slice(h - HALO, h)}

    def halo(dr, dc):
        i = (dr + 1) * 3 + dc + 1
        if dc:
            src = sent.at[(dc + 1) // 2, part_src[dr]]
            dst = got.at[(1 - dc) // 2, row_dst[dr]]
        else:
            src, dst = rows_sent.at[(dr + 1) // 2], rows_got.at[(1 - dr) // 2]
        return pltpu.make_async_remote_copy(
            src_ref=src,
            dst_ref=dst,
            send_sem=halo_send.at[i],
            recv_sem=halo_recv.at[i],
            device_id=device(t + dr, dc),
            device_id_type=MESH,
        )

    ways = [(0, -1), (0, 1), (-1, -1), (-1, 1), (1, -1), (1, 1), (-1, 0), (1, 0)]
    for dr, dc in ways:
        @when(rowhas[dr], has[dc])
        def _(dr=dr, dc=dc):
            halo(dr, dc).start()

    def gather(own, side, pack, send, recv, dt, dc):
        if dc:
            src, dst = pack.at[(dc + 1) // 2], side.at[t, (1 - dc) // 2]
        else:
            src, dst = own.at[t], own.at[t]
        return pltpu.make_async_remote_copy(
            src_ref=src,
            dst_ref=dst,
            send_sem=send.at[dt, dc + 1],
            recv_sem=recv.at[t, 1 - dc],
            device_id=device(lax.rem(t + dt, T), dc),
            device_id_type=MESH,
        )

    def arrival(own, side, pack, send, recv, dt, dc):
        s = lax.rem(t + dt, T)
        dst = side.at[s, (dc + 1) // 2] if dc else own.at[s]
        return pltpu.make_async_remote_copy(
            src_ref=dst,
            dst_ref=dst,
            send_sem=send.at[dt, dc + 1],
            recv_sem=recv.at[s, dc + 1],
            device_id=device(s, dc),
            device_id_type=MESH,
        )

    coef = (coef_own, coef_side, coef_pack, coef_send, coef_recv)
    src = (src_own, src_side, src_pack, src_send, src_recv)

    def scatter(x, way):
        own, pack = way[0], way[2]
        n = x.shape[0] // 2
        low = iota((n, SIDE), 1) < 64
        own[t] = x
        pack[0] = jnp.where(low, x[:n], pltpu.roll(x[n:], 64, 1))
        pack[1] = jnp.where(low, pltpu.roll(x[:n], 64, 1), x[n:])
        for dt, dc in partners:
            @when(has[dc])
            def _(dt=dt, dc=dc):
                gather(*way, dt, dc).start()

    def assemble(way, channel, count):
        for dt, dc in partners:
            @when(has[dc])
            def _(dt=dt, dc=dc):
                arrival(*way, dt, dc).wait_recv()
        own, side = way[:2]
        n = side.shape[2]
        low = iota((n, SIDE), 1) < 64

        def beside(s):
            left, right = side[s, 0], side[s, 1]
            return jnp.concatenate(
                [jnp.where(low, right, pltpu.roll(left, 64, 1)), jnp.where(low, pltpu.roll(right, 64, 1), left)], 0
            )

        for j in range(T // 2):
            for c in range(2):
                one, two = (beside(2 * j), beside(2 * j + 1)) if c else (own[2 * j], own[2 * j + 1])
                for i in range(count):
                    a2[channel + i, 8 * j : 8 * j + 8, SIDE * c : SIDE * c + SIDE] = jnp.concatenate(
                        [one[4 * i : 4 * i + 4], two[4 * i : 4 * i + 4]], 0
                    )

    even, odd = pool_matrix(256, 128), pool_matrix(256, 128, odd=True)
    even_ring, odd_ring = ring_pool(64), ring_pool(64, odd=True)
    wide = spread_matrix(128, 256)

    fine = [a0[3 + i, own_rows, own_cols] for i in range(8)]
    mid = coarsen_coefficients(fine, st, even, odd)
    for i in range(8):
        put(a1, 3 + i, 8, mid[i])
    mid = [jnp.concatenate(parts, 1) for parts in mid]
    low = [parts[0] for parts in coarsen_coefficients(mid, st, even, odd)]
    scatter(jnp.concatenate(low, 0), coef)

    for dr, dc in ways:
        if dc:
            @when(rowhas[dr], has[dc])
            def _(dr=dr, dc=dc):
                halo(-dr, -dc).wait_recv()

    for q in range(a0.shape[1] // 8):
        rows = slice(8 * q, 8 * q + 8)
        for i in range(11):
            right = pltpu.roll(got[1, rows], SIDE - DEEP * i, 1) if i else got[1, rows]
            left = pltpu.roll(got[0, rows], SIDE - DEEP - DEEP * i, 1)
            a0[i, rows, w : w + SIDE] = jnp.where(
                lane < DEEP, right, jnp.where(lane >= SIDE - DEEP, left, 0.0)
            )

    ends = [a0[3 + i, :, w : w + SIDE] for i in range(8)]
    for i, parts in enumerate(coarsen_coefficients(ends, st, even_ring, odd_ring)):
        put(a1, 3 + i, 4, parts, 2)

    for dr in (-1, 1):
        @when(rowhas[dr])
        def _(dr=dr):
            halo(-dr, 0).wait_recv()
            at = 0
            for i, n in enumerate(NEAR_ROWS):
                top = HALO - n if dr < 0 else HALO + h
                a0[i, top : top + n, own_cols] = rows_got[(dr + 1) // 2, at : at + n]
                at += n

    setup(a0, w0)
    first(a0, w0, x0)
    sweep(a0, w0, x0, u0)
    residual(a0, w0, u0, r0)
    source = pool_rows(pool_lanes(r0[...], even, even_ring), st)
    h1 = a0.shape[1] // 2
    for k in range(3):
        put(a1, k, 4, [p[k * h1 : k * h1 + h1] for p in source])
    beside = [
        jnp.concatenate([a0[3 + i, 0:HALO, own_cols], a0[3 + i, HALO + h :, own_cols]], 0) for i in range(8)
    ]
    for i, parts in enumerate(coarsen_coefficients(beside, st, even, odd)):
        put(a1, 3 + i, 4, [p[:4] for p in parts])
        put(a1, 3 + i, 16, [p[4:] for p in parts])
    setup(a1, w1)
    first(a1, w1, x1)
    sweep(a1, w1, x1, u1)
    residual(a1, w1, u1, r1)
    own = dot(r1[:, 0:256], even)
    source = pool_rows([own], st)[0]
    packed = [source[12 * k + 4 : 12 * k + 8] for k in range(3)]
    scatter(jnp.concatenate(packed + [jnp.zeros((4, SIDE), F32)], 0), src)

    def rows_copy(dr):
        i = (dr + 1) // 2
        return pltpu.make_async_remote_copy(
            src_ref=u1.at[:, 16:24, :],
            dst_ref=side_rows.at[1 - i],
            send_sem=row_send.at[i],
            recv_sem=row_recv.at[1 - i],
            device_id=device(t + dr, 0),
            device_id_type=MESH,
        )

    for dr in (-1, 1):
        @when(rowhas[dr])
        def _(dr=dr):
            rows_copy(dr).start()

    assemble(coef, 3, 8)
    setup(a2, w2)
    last, last_odd = ring_pool(96), ring_pool(96, odd=True)
    for a, b, aux, p, p_odd in ((a2, a3, w3, even, odd), (a3, a4, w4, last, last_odd)):
        for i, parts in enumerate(coarsen_coefficients([a[3 + i] for i in range(8)], st, p, p_odd)):
            put(b, 3 + i, 0, parts)
        setup(b, aux)
    assemble(src, 0, 3)

    for a, aux, x, u, r, b, p in ((a2, w2, x2, u2, r2, a3, even), (a3, w3, x3, u3, r3, a4, last)):
        first(a, aux, x)
        sweep(a, aux, x, u)
        residual(a, aux, u, r)
        source = pool_rows(pool_lanes(r[...], p), st)
        n = a.shape[1] // 2
        for k in range(3):
            put(b, k, 0, [z[k * n : k * n + n] for z in source])
    first(a4, w4, x4)
    now, then = x4, u4
    for _ in range(COARSE_SWEEPS - 1):
        sweep(a4, w4, now, then)
        now, then = then, now
    coarse = now
    for a, aux, x, u in ((a3, w3, x3, u3), (a2, w2, x2, u2)):
        n = coarse.shape[1] - 16
        y = jnp.concatenate([coarse[k, 8 : 8 + n] for k in range(3)], 0)
        z = dot(y, wide if a is a2 else ring_spread(SIDE, SIDE, 96))
        parts = [z[:, b : b + SIDE] for b in range(0, z.shape[1], SIDE)]
        add_spread(u, x, spread_rows(parts, st), 2 * n, len(parts), a.shape[1])
        sweep(a, aux, x, u)
        sweep(a, aux, u, x)
        coarse = x

    for s in range(T):
        @pl.when(t == s)
        def _(s=s):
            for k in range(3):
                win[16 * k : 16 * k + 16, :] = x2[k, 4 + 4 * s : 20 + 4 * s]
    y = dot(win[...], ring_spread(256, 384, 320))
    spread = spread_rows([y[:, 128 * b : 128 * b + 128] for b in range(3)], st)
    for dr in (-1, 1):
        @when(rowhas[dr])
        def _(dr=dr):
            rows_copy(dr).wait_send()
            rows_copy(-dr).wait_recv()
    u1[:, 8:16, :] = side_rows[0]
    u1[:, 24:32, :] = side_rows[1]
    add_spread(u1, x1, spread, 32, 3, 24)
    sweep(a1, w1, x1, u1)
    sweep(a1, w1, u1, x1)

    y = jnp.concatenate([x1[k, 8:32] for k in range(3)], 0)
    parts = []
    for b in range(2):
        z = dot(y[:, 128 * b : 128 * b + 128], wide)
        parts += [z[:, :128], z[:, 128:]]
    parts.append(dot(y[:, 256:384], ring_spread(SIDE, SIDE, 64)))
    add_spread(u0, x0, spread_rows(parts, st), 48, 5, 32, row0=8)
    sweep(a0, w0, x0, u0)
    for q in range(1, 1 + h // 8):
        mid, res = residual_at(a0, w0, u0, q)
        for k in range(3):
            new = mid[k] + w0[3 + k, 8 * q : 8 * q + 8] * res[k]
            out[k, 8 * q - 8 : 8 * q, :] = new[:, own_cols]

    for dr, dc in ways:
        @when(rowhas[dr], has[dc])
        def _(dr=dr, dc=dc):
            halo(dr, dc).wait_send()
    for dt, dc in partners:
        @when(has[dc])
        def _(dt=dt, dc=dc):
            gather(*coef, dt, dc).wait_send()
            gather(*src, dt, dc).wait_send()


def on_device(right_side, noise_block, edges):
    T, NB, NS = lax.axis_size("tiles"), lax.axis_size("band"), lax.axis_size("stokes")
    _, h, w = right_side.shape
    shapes = [
        (h + 2 * HALO, w + SIDE),
        (h // 2 + 16, w // 2 + SIDE),
        (h // 4 * T, 2 * SIDE),
        (max(8, h // 8 * T), SIDE),
        (max(8, h // 16 * T), SIDE),
    ]
    scratch = []
    for i, (n, m) in enumerate(shapes):
        scratch += [
            pltpu.VMEM((11, n, m), F32),
            pltpu.VMEM((3, n + 16, m), F32),
            pltpu.VMEM((3, n + 16, m), F32),
            pltpu.VMEM((6, n, m), F32),
        ]
        if i < 4:
            scratch.append(pltpu.VMEM((3 * n, m), F32))
    scratch += [
        pltpu.VMEM((BUFFERS, 5, max(6 * 32, 6 * h // 4 * T), SIDE), F32),
        pltpu.VMEM((48, 2 * SIDE), F32),
        pltpu.VMEM((2, h, SIDE), F32),
        pltpu.VMEM((2, h + 2 * HALO, SIDE), F32),
        pltpu.VMEM((2, sum(NEAR_ROWS), w), F32),
        pltpu.VMEM((2, sum(NEAR_ROWS), w), F32),
        pltpu.VMEM((T, 32, SIDE), F32),
        pltpu.VMEM((T, 2, 16, SIDE), F32),
        pltpu.VMEM((2, 16, SIDE), F32),
        pltpu.VMEM((T, 16, SIDE), F32),
        pltpu.VMEM((T, 2, 8, SIDE), F32),
        pltpu.VMEM((2, 8, SIDE), F32),
        pltpu.VMEM((2, 3, 8, 3 * SIDE), F32),
        pltpu.SemaphoreType.DMA((1,)),
        pltpu.SemaphoreType.DMA((9,)),
        pltpu.SemaphoreType.DMA((9,)),
        pltpu.SemaphoreType.DMA((T, 3)),
        pltpu.SemaphoreType.DMA((T, 3)),
        pltpu.SemaphoreType.DMA((T, 3)),
        pltpu.SemaphoreType.DMA((T, 3)),
        pltpu.SemaphoreType.DMA((2,)),
        pltpu.SemaphoreType.DMA((2,)),
    ]
    return pl.pallas_call(
        functools.partial(kernel, T, NB, NS),
        out_shape=jax.ShapeDtypeStruct(right_side.shape, F32),
        in_specs=[pl.BlockSpec(memory_space=pltpu.VMEM)],
        out_specs=pl.BlockSpec(memory_space=pltpu.VMEM),
        scratch_shapes=scratch,
        compiler_params=pltpu.CompilerParams(
            collective_id=0, has_side_effects=True, vmem_limit_bytes=40 * 1024 * 1024
        ),
    )(jnp.concatenate([right_side, noise_block, edges], 0))


def solution(mesh):
    spec = P(None, ("groups", "tiles"), ("band", "stokes"))
    return jax.shard_map(
        on_device, mesh=mesh, in_specs=(spec, spec, spec), out_specs=spec, check_vma=False
    )
```

```python
import functools
import itertools

import jax
import jax.numpy as jnp
from jax import lax
from jax.experimental import pallas as pl
from jax.experimental.pallas import tpu as pltpu
from jax.sharding import PartitionSpec as P

OMEGA = 0.8
COARSE_SWEEPS = 8
HALO = 8
SIDE = 128
DEEP = 11
BUFFERS = 12
NEAR_ROWS = (6, 6, 6, 6, 6, 6, 5, 5, 5, 7, 6)
MESH = pl.DeviceIdType.MESH
F32 = jnp.float32


def rounded(x):
    return x.astype(jnp.bfloat16).astype(F32)


def dot(x, y):
    n = x.shape[0]
    high = rounded(x)
    pieces = jnp.concatenate([high, x - high], 0)
    z = jnp.dot(pieces, y, precision=lax.Precision.DEFAULT, preferred_element_type=F32)
    return z[:n] + z[n:]


def iota(shape, dim):
    return lax.broadcasted_iota(jnp.int32, shape, dim)


def ones(hit):
    return jnp.where(hit, 1.0, 0.0).astype(F32)


def half(i):
    return lax.shift_right_logical(i, 1)


def pool_matrix(n, m, odd=False):
    c, j = iota((n, m), 0), iota((n, m), 1)
    hit = c == 2 * j + 1
    return ones(hit if odd else hit | (c == 2 * j))


def spread_matrix(n, m):
    c, j = iota((n, m), 0), iota((n, m), 1)
    return ones(c == half(j))


def ring_pool(cut, odd=False):
    c, j = iota((SIDE, SIDE), 0), iota((SIDE, SIDE), 1)
    hit = j == half(c) + jnp.where(c >= cut, 64, 0)
    return ones(hit & ((c & 1) == 1) if odd else hit)


def ring_spread(n, m, cut):
    c, j = iota((n, m), 0), iota((n, m), 1)
    return ones(c == half(j) + jnp.where(j >= cut, 64, 0))


def chunks(a):
    return range(a.shape[1] // 8)


def setup(a, aux):
    for q in chunks(a):
        rows = slice(8 * q, 8 * q + 8)
        down, right = a[9, rows], a[10, rows]
        if q == 0:
            up = jnp.where(iota(down.shape, 0) == 0, 0.0, pltpu.roll(down, 1, 0))
        else:
            up = a[9, 8 * q - 1 : 8 * q + 7]
        left = pltpu.roll(right, 1, 1)
        total = down + up + right + left
        aux[0, rows], aux[1, rows], aux[2, rows] = up, left, total
        for k in range(3):
            aux[3 + k, rows] = jnp.where(down > 0, OMEGA / (a[3 + k, rows] + total), 0.0)


def first(a, aux, v):
    for q in chunks(a):
        rows = slice(8 * q, 8 * q + 8)
        for k in range(3):
            v[k, 8 + 8 * q : 16 + 8 * q] = aux[3 + k, rows] * a[k, rows]


def residual_at(a, aux, v, q):
    rows = slice(8 * q, 8 * q + 8)
    mid = [v[k, 8 + 8 * q : 16 + 8 * q] for k in range(3)]
    n = [a[3 + i, rows] for i in range(6)]
    down, right, up, left, total = a[9, rows], a[10, rows], aux[0, rows], aux[1, rows], aux[2, rows]
    width = mid[0].shape[1]
    image = [
        n[0] * mid[0] + n[3] * mid[1] + n[4] * mid[2],
        n[3] * mid[0] + n[1] * mid[1] + n[5] * mid[2],
        n[4] * mid[0] + n[5] * mid[1] + n[2] * mid[2],
    ]
    out = []
    for k in range(3):
        near = (
            down * v[k, 9 + 8 * q : 17 + 8 * q]
            + up * v[k, 7 + 8 * q : 15 + 8 * q]
            + right * pltpu.roll(mid[k], width - 1, 1)
            + left * pltpu.roll(mid[k], 1, 1)
        )
        out.append(a[k, rows] - (image[k] + total * mid[k] - near))
    return mid, out


def sweep(a, aux, src, dst, which=None):
    for q in chunks(a) if which is None else which:
        mid, res = residual_at(a, aux, src, q)
        for k in range(3):
            dst[k, 8 + 8 * q : 16 + 8 * q] = mid[k] + aux[3 + k, 8 * q : 8 * q + 8] * res[k]


def residual(a, aux, v, r):
    height = a.shape[1]
    for q in chunks(a):
        _, res = residual_at(a, aux, v, q)
        for k in range(3):
            r[k * height + 8 * q : k * height + 8 * q + 8, :] = res[k]


def pool_lanes(x, matrix, tail=None):
    n = matrix.shape[0]
    width = x.shape[1]
    parts = []
    for b in range(0, width, n):
        if b + n <= width:
            parts.append(dot(x[:, b : b + n], matrix))
        else:
            parts.append(dot(x[:, b:width], matrix[: width - b] if tail is None else tail))
    return parts


def pool_rows(parts, st, odd=False):
    st = st()
    out = []
    for b, part in enumerate(parts):
        n = part.shape[0]
        st[b, 0:n, :] = part
        top = st[b, pl.ds(1, n // 2, stride=2), :]
        out.append(top if odd else top + st[b, pl.ds(0, n // 2, stride=2), :])
    return out


def coarsen_coefficients(arrays, st, even, odd):
    h = arrays[0].shape[0]
    parts = pool_lanes(jnp.concatenate(arrays[:7], 0), even)
    noise = pool_rows([p[: 6 * h] for p in parts], st)
    down = pool_rows([p[6 * h :] for p in parts], st, odd=True)
    right = pool_rows(pool_lanes(arrays[7], odd), st)
    h = h // 2
    out = []
    for i in range(6):
        out.append([p[i * h : i * h + h] for p in noise])
    return out + [down, right]


def spread_rows(parts, st):
    st = st()
    for b, part in enumerate(parts):
        n = part.shape[0]
        st[b, pl.ds(0, n, stride=2), :] = part
        st[b, pl.ds(1, n, stride=2), :] = part
    return st


def put(a, channel, row, parts, tile=0):
    for b, part in enumerate(parts, tile):
        a[channel, row : row + part.shape[0], SIDE * b : SIDE * b + SIDE] = part


def add_spread(v, dst, st, stride, blocks, height, row0=0):
    for k in range(3):
        for b in range(blocks):
            lanes = slice(SIDE * b, SIDE * b + SIDE)
            dst[k, 8 : 8 + height, lanes] = v[k, 8 : 8 + height, lanes] + st[b, stride * k + row0 : stride * k + row0 + height, :]


def kernel(
    T, NB, NS, stack, out,
    a0, x0, u0, w0, r0, a1, x1, u1, w1, r1, a2, x2, u2, w2, r2, a3, x3, u3, w3, r3, a4, x4, u4, w4,
    tiles, win, sent, got, rows_sent, rows_got,
    coef_own, coef_side, coef_pack, src_own, src_side, src_pack, side_rows,
    in_sem, halo_send, halo_recv, coef_send, coef_recv, src_send, src_recv, row_send, row_recv,
):
    turn = itertools.cycle(range(BUFFERS))

    def st():
        return tiles.at[next(turn)]

    t = lax.axis_index("tiles")
    col = lax.axis_index("band") * NS + lax.axis_index("stokes")
    cols = NB * NS
    h, w = stack.shape[1], stack.shape[2]
    has = {-1: col > 0, 0: None, 1: col < cols - 1}
    rowhas = {-1: t > 0, 0: None, 1: t < T - 1}

    def when(*conds):
        conds = [c for c in conds if c is not None]
        if not conds:
            return lambda f: f()
        return pl.when(functools.reduce(jnp.logical_and, conds))

    def device(tile, dc):
        c = col + dc
        return {"tiles": tile, "band": c // NS, "stokes": lax.rem(c, NS)}

    own_rows, own_cols = slice(HALO, HALO + h), slice(0, w)
    load = pltpu.make_async_copy(stack, a0.at[:, own_rows, own_cols], in_sem.at[0])
    load.start()

    partners = [(dt, dc) for dc in (-1, 0, 1) for dt in range(T) if dt or dc]
    barrier = pltpu.get_barrier_semaphore()
    for dt, dc in partners:
        @when(has[dc])
        def _(dt=dt, dc=dc):
            pl.semaphore_signal(barrier, inc=1, device_id=device(lax.rem(t + dt, T), dc), device_id_type=MESH)

    @pl.when(t == 0)
    def _():
        got[:, 0:HALO] = jnp.zeros_like(got[:, 0:HALO])
        side_rows[0] = jnp.zeros_like(side_rows[0])

    @pl.when(t == T - 1)
    def _():
        got[:, HALO + h :] = jnp.zeros_like(got[:, HALO + h :])
        side_rows[1] = jnp.zeros_like(side_rows[1])

    @pl.when(col == 0)
    def _():
        got[0] = jnp.zeros_like(got[0])
        coef_side[:, 0] = jnp.zeros_like(coef_side[:, 0])
        src_side[:, 0] = jnp.zeros_like(src_side[:, 0])

    @pl.when(col == cols - 1)
    def _():
        got[1] = jnp.zeros_like(got[1])
        coef_side[:, 1] = jnp.zeros_like(coef_side[:, 1])
        src_side[:, 1] = jnp.zeros_like(src_side[:, 1])

    a0[:, 0:HALO, own_cols] = jnp.zeros_like(a0[:, 0:HALO, own_cols])
    a0[:, HALO + h :, own_cols] = jnp.zeros_like(a0[:, HALO + h :, own_cols])
    for a in (a1, a3, a4):
        a[...] = jnp.zeros_like(a)
    for v in (x0, u0, x1, u1, x2, u2, x3, u3, x4, u4):
        v[:, 0:8, :] = jnp.zeros_like(v[:, 0:8, :])
        n = v.shape[1]
        v[:, n - 8 : n, :] = jnp.zeros_like(v[:, n - 8 : n, :])

    load.wait()

    lane = iota((8, SIDE), 1)
    for q in range(h // 8):
        rows = slice(HALO + 8 * q, HALO + 8 * q + 8)
        head = tail = jnp.zeros((8, SIDE), F32)
        for i in range(11):
            here = (lane >= DEEP * i) & (lane < DEEP * i + DEEP)
            one, two = a0[i, rows, 0:SIDE], a0[i, rows, w - SIDE : w]
            head = jnp.where(here, pltpu.roll(one, DEEP * i, 1) if i else one, head)
            tail = jnp.where(here, pltpu.roll(two, (DEEP * i + DEEP) % SIDE, 1), tail)
        sent[0, 8 * q : 8 * q + 8], sent[1, 8 * q : 8 * q + 8] = head, tail
    at = 0
    for i, n in enumerate(NEAR_ROWS):
        rows_sent[0, at : at + n] = a0[i, HALO : HALO + n, own_cols]
        rows_sent[1, at : at + n] = a0[i, HALO + h - n : HALO + h, own_cols]
        at += n

    sides = 1 + jnp.where(col > 0, 1, 0) + jnp.where(col < cols - 1, 1, 0)
    pl.semaphore_wait(barrier, sides * T - 1)

    row_dst = {-1: slice(HALO + h, 2 * HALO + h), 0: own_rows, 1: slice(0, HALO)}
    part_src = {-1: slice(0, HALO), 0: slice(0, h), 1: slice(h - HALO, h)}

    def halo(dr, dc):
        i = (dr + 1) * 3 + dc + 1
        if dc:
            src = sent.at[(dc + 1) // 2, part_src[dr]]
            dst = got.at[(1 - dc) // 2, row_dst[dr]]
        else:
            src, dst = rows_sent.at[(dr + 1) // 2], rows_got.at[(1 - dr) // 2]
        return pltpu.make_async_remote_copy(
            src_ref=src,
            dst_ref=dst,
            send_sem=halo_send.at[i],
            recv_sem=halo_recv.at[i],
            device_id=device(t + dr, dc),
            device_id_type=MESH,
        )

    ways = [(0, -1), (0, 1), (-1, -1), (-1, 1), (1, -1), (1, 1), (-1, 0), (1, 0)]
    for dr, dc in ways:
        @when(rowhas[dr], has[dc])
        def _(dr=dr, dc=dc):
            halo(dr, dc).start()

    def gather(own, side, pack, send, recv, dt, dc):
        if dc:
            src, dst = pack.at[(dc + 1) // 2], side.at[t, (1 - dc) // 2]
        else:
            src, dst = own.at[t], own.at[t]
        return pltpu.make_async_remote_copy(
            src_ref=src,
            dst_ref=dst,
            send_sem=send.at[dt, dc + 1],
            recv_sem=recv.at[t, 1 - dc],
            device_id=device(lax.rem(t + dt, T), dc),
            device_id_type=MESH,
        )

    def arrival(own, side, pack, send, recv, dt, dc):
        s = lax.rem(t + dt, T)
        dst = side.at[s, (dc + 1) // 2] if dc else own.at[s]
        return pltpu.make_async_remote_copy(
            src_ref=dst,
            dst_ref=dst,
            send_sem=send.at[dt, dc + 1],
            recv_sem=recv.at[s, dc + 1],
            device_id=device(s, dc),
            device_id_type=MESH,
        )

    coef = (coef_own, coef_side, coef_pack, coef_send, coef_recv)
    src = (src_own, src_side, src_pack, src_send, src_recv)

    def scatter(x, way):
        own, pack = way[0], way[2]
        n = x.shape[0] // 2
        low = iota((n, SIDE), 1) < 64
        own[t] = x
        pack[0] = jnp.where(low, x[:n], pltpu.roll(x[n:], 64, 1))
        pack[1] = jnp.where(low, pltpu.roll(x[:n], 64, 1), x[n:])
        for dt, dc in partners:
            @when(has[dc])
            def _(dt=dt, dc=dc):
                gather(*way, dt, dc).start()

    def assemble(way, channel, count):
        for dt, dc in partners:
            @when(has[dc])
            def _(dt=dt, dc=dc):
                arrival(*way, dt, dc).wait_recv()
        own, side = way[:2]
        n = side.shape[2]
        low = iota((n, SIDE), 1) < 64

        def beside(s):
            left, right = side[s, 0], side[s, 1]
            return jnp.concatenate(
                [jnp.where(low, right, pltpu.roll(left, 64, 1)), jnp.where(low, pltpu.roll(right, 64, 1), left)], 0
            )

        for j in range(T // 2):
            for c in range(2):
                one, two = (beside(2 * j), beside(2 * j + 1)) if c else (own[2 * j], own[2 * j + 1])
                for i in range(count):
                    a2[channel + i, 8 * j : 8 * j + 8, SIDE * c : SIDE * c + SIDE] = jnp.concatenate(
                        [one[4 * i : 4 * i + 4], two[4 * i : 4 * i + 4]], 0
                    )

    even, odd = pool_matrix(256, 128), pool_matrix(256, 128, odd=True)
    even_ring, odd_ring = ring_pool(64), ring_pool(64, odd=True)
    wide = spread_matrix(128, 256)

    fine = [a0[3 + i, own_rows, own_cols] for i in range(8)]
    mid = coarsen_coefficients(fine, st, even, odd)
    for i in range(8):
        put(a1, 3 + i, 8, mid[i])
    mid = [jnp.concatenate(parts, 1) for parts in mid]
    low = [parts[0] for parts in coarsen_coefficients(mid, st, even, odd)]
    scatter(jnp.concatenate(low, 0), coef)

    for dr, dc in ways:
        if dc:
            @when(rowhas[dr], has[dc])
            def _(dr=dr, dc=dc):
                halo(-dr, -dc).wait_recv()

    for q in range(a0.shape[1] // 8):
        rows = slice(8 * q, 8 * q + 8)
        for i in range(11):
            right = pltpu.roll(got[1, rows], SIDE - DEEP * i, 1) if i else got[1, rows]
            left = pltpu.roll(got[0, rows], SIDE - DEEP - DEEP * i, 1)
            a0[i, rows, w : w + SIDE] = jnp.where(
                lane < DEEP, right, jnp.where(lane >= SIDE - DEEP, left, 0.0)
            )

    ends = [a0[3 + i, :, w : w + SIDE] for i in range(8)]
    for i, parts in enumerate(coarsen_coefficients(ends, st, even_ring, odd_ring)):
        put(a1, 3 + i, 4, parts, 2)

    for dr in (-1, 1):
        @when(rowhas[dr])
        def _(dr=dr):
            halo(-dr, 0).wait_recv()
            at = 0
            for i, n in enumerate(NEAR_ROWS):
                top = HALO - n if dr < 0 else HALO + h
                a0[i, top : top + n, own_cols] = rows_got[(dr + 1) // 2, at : at + n]
                at += n

    setup(a0, w0)
    first(a0, w0, x0)
    sweep(a0, w0, x0, u0)
    residual(a0, w0, u0, r0)
    source = pool_rows(pool_lanes(r0[...], even, even_ring), st)
    h1 = a0.shape[1] // 2
    for k in range(3):
        put(a1, k, 4, [p[k * h1 : k * h1 + h1] for p in source])
    beside = [
        jnp.concatenate([a0[3 + i, 0:HALO, own_cols], a0[3 + i, HALO + h :, own_cols]], 0) for i in range(8)
    ]
    for i, parts in enumerate(coarsen_coefficients(beside, st, even, odd)):
        put(a1, 3 + i, 4, [p[:4] for p in parts])
        put(a1, 3 + i, 16, [p[4:] for p in parts])
    setup(a1, w1)
    first(a1, w1, x1)
    sweep(a1, w1, x1, u1)
    residual(a1, w1, u1, r1)
    own = dot(r1[:, 0:256], even)
    source = pool_rows([own], st)[0]
    packed = [source[12 * k + 4 : 12 * k + 8] for k in range(3)]
    scatter(jnp.concatenate(packed + [jnp.zeros((4, SIDE), F32)], 0), src)

    def rows_copy(dr):
        i = (dr + 1) // 2
        return pltpu.make_async_remote_copy(
            src_ref=u1.at[:, 16:24, :],
            dst_ref=side_rows.at[1 - i],
            send_sem=row_send.at[i],
            recv_sem=row_recv.at[1 - i],
            device_id=device(t + dr, 0),
            device_id_type=MESH,
        )

    for dr in (-1, 1):
        @when(rowhas[dr])
        def _(dr=dr):
            rows_copy(dr).start()

    assemble(coef, 3, 8)
    setup(a2, w2)
    last, last_odd = ring_pool(96), ring_pool(96, odd=True)
    for a, b, aux, p, p_odd in ((a2, a3, w3, even, odd), (a3, a4, w4, last, last_odd)):
        for i, parts in enumerate(coarsen_coefficients([a[3 + i] for i in range(8)], st, p, p_odd)):
            put(b, 3 + i, 0, parts)
        setup(b, aux)
    assemble(src, 0, 3)

    for a, aux, x, u, r, b, p in ((a2, w2, x2, u2, r2, a3, even), (a3, w3, x3, u3, r3, a4, last)):
        first(a, aux, x)
        sweep(a, aux, x, u)
        residual(a, aux, u, r)
        source = pool_rows(pool_lanes(r[...], p), st)
        n = a.shape[1] // 2
        for k in range(3):
            put(b, k, 0, [z[k * n : k * n + n] for z in source])
    if h // 16 * T < 8:
        n = [a4[3 + i] for i in range(6)]
        down, right, up, left, total = a4[9], a4[10], w4[0], w4[1], w4[2]
        source, scale = [a4[k] for k in range(3)], [w4[3 + k] for k in range(3)]
        v = [scale[k] * source[k] for k in range(3)]
        weight = [n[k] + total for k in range(3)]
        for _ in range(COARSE_SWEEPS - 1):
            cross = [n[3] * v[1] + n[4] * v[2], n[3] * v[0] + n[5] * v[2], n[4] * v[0] + n[5] * v[1]]
            new = []
            for k in range(3):
                near = (down * pltpu.roll(v[k], 7, 0) + up * pltpu.roll(v[k], 1, 0)) + (
                    right * pltpu.roll(v[k], SIDE - 1, 1) + left * pltpu.roll(v[k], 1, 1)
                )
                new.append(v[k] + scale[k] * (source[k] - (weight[k] * v[k] + cross[k]) + near))
            v = new
    else:
        first(a4, w4, x4)
        now, then = x4, u4
        for _ in range(COARSE_SWEEPS - 1):
            sweep(a4, w4, now, then)
            now, then = then, now
        v = [now[k, 8 : 8 + a4.shape[1]] for k in range(3)]
    for a, aux, x, u in ((a3, w3, x3, u3), (a2, w2, x2, u2)):
        n = v[0].shape[0]
        z = dot(jnp.concatenate(v, 0), wide if a is a2 else ring_spread(SIDE, SIDE, 96))
        parts = [z[:, b : b + SIDE] for b in range(0, z.shape[1], SIDE)]
        add_spread(u, x, spread_rows(parts, st), 2 * n, len(parts), a.shape[1])
        sweep(a, aux, x, u)
        sweep(a, aux, u, x)
        v = [x[k, 8 : 8 + a.shape[1]] for k in range(3)]

    for s in range(T):
        @pl.when(t == s)
        def _(s=s):
            for k in range(3):
                win[16 * k : 16 * k + 16, :] = x2[k, 4 + 4 * s : 20 + 4 * s]
    y = dot(win[...], ring_spread(256, 384, 320))
    spread = spread_rows([y[:, 128 * b : 128 * b + 128] for b in range(3)], st)
    for dr in (-1, 1):
        @when(rowhas[dr])
        def _(dr=dr):
            rows_copy(dr).wait_send()
            rows_copy(-dr).wait_recv()
    u1[:, 8:16, :] = side_rows[0]
    u1[:, 24:32, :] = side_rows[1]
    add_spread(u1, x1, spread, 32, 3, 24)
    sweep(a1, w1, x1, u1)
    sweep(a1, w1, u1, x1)

    y = jnp.concatenate([x1[k, 8:32] for k in range(3)], 0)
    parts = []
    for b in range(2):
        z = dot(y[:, 128 * b : 128 * b + 128], wide)
        parts += [z[:, :128], z[:, 128:]]
    parts.append(dot(y[:, 256:384], ring_spread(SIDE, SIDE, 64)))
    add_spread(u0, x0, spread_rows(parts, st), 48, 5, 32, row0=8)
    sweep(a0, w0, x0, u0)
    for q in range(1, 1 + h // 8):
        mid, res = residual_at(a0, w0, u0, q)
        for k in range(3):
            new = mid[k] + w0[3 + k, 8 * q : 8 * q + 8] * res[k]
            out[k, 8 * q - 8 : 8 * q, :] = new[:, own_cols]

    for dr, dc in ways:
        @when(rowhas[dr], has[dc])
        def _(dr=dr, dc=dc):
            halo(dr, dc).wait_send()
    for dt, dc in partners:
        @when(has[dc])
        def _(dt=dt, dc=dc):
            gather(*coef, dt, dc).wait_send()
            gather(*src, dt, dc).wait_send()


def on_device(right_side, noise_block, edges):
    T, NB, NS = lax.axis_size("tiles"), lax.axis_size("band"), lax.axis_size("stokes")
    _, h, w = right_side.shape
    shapes = [
        (h + 2 * HALO, w + SIDE),
        (h // 2 + 16, w // 2 + SIDE),
        (h // 4 * T, 2 * SIDE),
        (max(8, h // 8 * T), SIDE),
        (max(8, h // 16 * T), SIDE),
    ]
    scratch = []
    for i, (n, m) in enumerate(shapes):
        scratch += [
            pltpu.VMEM((11, n, m), F32),
            pltpu.VMEM((3, n + 16, m), F32),
            pltpu.VMEM((3, n + 16, m), F32),
            pltpu.VMEM((6, n, m), F32),
        ]
        if i < 4:
            scratch.append(pltpu.VMEM((3 * n, m), F32))
    scratch += [
        pltpu.VMEM((BUFFERS, 5, max(6 * 32, 6 * h // 4 * T), SIDE), F32),
        pltpu.VMEM((48, 2 * SIDE), F32),
        pltpu.VMEM((2, h, SIDE), F32),
        pltpu.VMEM((2, h + 2 * HALO, SIDE), F32),
        pltpu.VMEM((2, sum(NEAR_ROWS), w), F32),
        pltpu.VMEM((2, sum(NEAR_ROWS), w), F32),
        pltpu.VMEM((T, 32, SIDE), F32),
        pltpu.VMEM((T, 2, 16, SIDE), F32),
        pltpu.VMEM((2, 16, SIDE), F32),
        pltpu.VMEM((T, 16, SIDE), F32),
        pltpu.VMEM((T, 2, 8, SIDE), F32),
        pltpu.VMEM((2, 8, SIDE), F32),
        pltpu.VMEM((2, 3, 8, 3 * SIDE), F32),
        pltpu.SemaphoreType.DMA((1,)),
        pltpu.SemaphoreType.DMA((9,)),
        pltpu.SemaphoreType.DMA((9,)),
        pltpu.SemaphoreType.DMA((T, 3)),
        pltpu.SemaphoreType.DMA((T, 3)),
        pltpu.SemaphoreType.DMA((T, 3)),
        pltpu.SemaphoreType.DMA((T, 3)),
        pltpu.SemaphoreType.DMA((2,)),
        pltpu.SemaphoreType.DMA((2,)),
    ]
    return pl.pallas_call(
        functools.partial(kernel, T, NB, NS),
        out_shape=jax.ShapeDtypeStruct(right_side.shape, F32),
        in_specs=[pl.BlockSpec(memory_space=pltpu.VMEM)],
        out_specs=pl.BlockSpec(memory_space=pltpu.VMEM),
        scratch_shapes=scratch,
        compiler_params=pltpu.CompilerParams(
            collective_id=0, has_side_effects=True, vmem_limit_bytes=40 * 1024 * 1024
        ),
    )(jnp.concatenate([right_side, noise_block, edges], 0))


def solution(mesh):
    spec = P(None, ("groups", "tiles"), ("band", "stokes"))
    return jax.shard_map(
        on_device, mesh=mesh, in_specs=(spec, spec, spec), out_specs=spec, check_vma=False
    )
```

```python
import functools
import itertools

import jax
import jax.numpy as jnp
from jax import lax
from jax.experimental import pallas as pl
from jax.experimental.pallas import tpu as pltpu
from jax.sharding import PartitionSpec as P

OMEGA = 0.8
COARSE_SWEEPS = 8
HALO = 8
SIDE = 128
DEEP = 11
BUFFERS = 12
NEAR_ROWS = (6, 6, 6, 6, 6, 6, 5, 5, 5, 7, 6)
MESH = pl.DeviceIdType.MESH
F32 = jnp.float32


def rounded(x):
    return x.astype(jnp.bfloat16).astype(F32)


def dot(x, y):
    n = x.shape[0]
    high = rounded(x)
    pieces = jnp.concatenate([high, x - high], 0)
    z = jnp.dot(pieces, y, precision=lax.Precision.DEFAULT, preferred_element_type=F32)
    return z[:n] + z[n:]


def iota(shape, dim):
    return lax.broadcasted_iota(jnp.int32, shape, dim)


def ones(hit):
    return jnp.where(hit, 1.0, 0.0).astype(F32)


def half(i):
    return lax.shift_right_logical(i, 1)


def pool_matrix(n, m, odd=False):
    c, j = iota((n, m), 0), iota((n, m), 1)
    hit = c == 2 * j + 1
    return ones(hit if odd else hit | (c == 2 * j))


def spread_matrix(n, m):
    c, j = iota((n, m), 0), iota((n, m), 1)
    return ones(c == half(j))


def ring_pool(cut, odd=False):
    c, j = iota((SIDE, SIDE), 0), iota((SIDE, SIDE), 1)
    hit = j == half(c) + jnp.where(c >= cut, 64, 0)
    return ones(hit & ((c & 1) == 1) if odd else hit)


def ring_spread(n, m, cut):
    c, j = iota((n, m), 0), iota((n, m), 1)
    return ones(c == half(j) + jnp.where(j >= cut, 64, 0))


def chunks(a):
    return range(a.shape[1] // 8)


def setup(a, aux):
    for q in chunks(a):
        rows = slice(8 * q, 8 * q + 8)
        down, right = a[9, rows], a[10, rows]
        if q == 0:
            up = jnp.where(iota(down.shape, 0) == 0, 0.0, pltpu.roll(down, 1, 0))
        else:
            up = a[9, 8 * q - 1 : 8 * q + 7]
        left = pltpu.roll(right, 1, 1)
        total = down + up + right + left
        aux[0, rows], aux[1, rows], aux[2, rows] = up, left, total
        for k in range(3):
            aux[3 + k, rows] = jnp.where(down > 0, OMEGA / (a[3 + k, rows] + total), 0.0)


def first(a, aux, v):
    for q in chunks(a):
        rows = slice(8 * q, 8 * q + 8)
        for k in range(3):
            v[k, 8 + 8 * q : 16 + 8 * q] = aux[3 + k, rows] * a[k, rows]


def residual_at(a, aux, v, q):
    rows = slice(8 * q, 8 * q + 8)
    mid = [v[k, 8 + 8 * q : 16 + 8 * q] for k in range(3)]
    n = [a[3 + i, rows] for i in range(6)]
    down, right, up, left, total = a[9, rows], a[10, rows], aux[0, rows], aux[1, rows], aux[2, rows]
    width = mid[0].shape[1]
    image = [
        n[0] * mid[0] + n[3] * mid[1] + n[4] * mid[2],
        n[3] * mid[0] + n[1] * mid[1] + n[5] * mid[2],
        n[4] * mid[0] + n[5] * mid[1] + n[2] * mid[2],
    ]
    out = []
    for k in range(3):
        near = (
            down * v[k, 9 + 8 * q : 17 + 8 * q]
            + up * v[k, 7 + 8 * q : 15 + 8 * q]
            + right * pltpu.roll(mid[k], width - 1, 1)
            + left * pltpu.roll(mid[k], 1, 1)
        )
        out.append(a[k, rows] - (image[k] + total * mid[k] - near))
    return mid, out


def sweep(a, aux, src, dst, which=None):
    for q in chunks(a) if which is None else which:
        mid, res = residual_at(a, aux, src, q)
        for k in range(3):
            dst[k, 8 + 8 * q : 16 + 8 * q] = mid[k] + aux[3 + k, 8 * q : 8 * q + 8] * res[k]


def residual(a, aux, v, r):
    height = a.shape[1]
    for q in chunks(a):
        _, res = residual_at(a, aux, v, q)
        for k in range(3):
            r[k * height + 8 * q : k * height + 8 * q + 8, :] = res[k]


def pool_lanes(x, matrix, tail=None):
    n = matrix.shape[0]
    width = x.shape[1]
    parts = []
    for b in range(0, width, n):
        if b + n <= width:
            parts.append(dot(x[:, b : b + n], matrix))
        else:
            parts.append(dot(x[:, b:width], matrix[: width - b] if tail is None else tail))
    return parts


def pool_rows(parts, st, odd=False):
    st = st()
    out = []
    for b, part in enumerate(parts):
        n = part.shape[0]
        st[b, 0:n, :] = part
        top = st[b, pl.ds(1, n // 2, stride=2), :]
        out.append(top if odd else top + st[b, pl.ds(0, n // 2, stride=2), :])
    return out


def coarsen_coefficients(arrays, st, even, odd):
    h = arrays[0].shape[0]
    parts = pool_lanes(jnp.concatenate(arrays[:7], 0), even)
    noise = pool_rows([p[: 6 * h] for p in parts], st)
    down = pool_rows([p[6 * h :] for p in parts], st, odd=True)
    right = pool_rows(pool_lanes(arrays[7], odd), st)
    h = h // 2
    out = []
    for i in range(6):
        out.append([p[i * h : i * h + h] for p in noise])
    return out + [down, right]


def spread_rows(parts, st):
    st = st()
    for b, part in enumerate(parts):
        n = part.shape[0]
        st[b, pl.ds(0, n, stride=2), :] = part
        st[b, pl.ds(1, n, stride=2), :] = part
    return st


def put(a, channel, row, parts, tile=0):
    for b, part in enumerate(parts, tile):
        a[channel, row : row + part.shape[0], SIDE * b : SIDE * b + SIDE] = part


def add_spread(v, dst, st, stride, blocks, height, row0=0):
    for k in range(3):
        for b in range(blocks):
            lanes = slice(SIDE * b, SIDE * b + SIDE)
            dst[k, 8 : 8 + height, lanes] = v[k, 8 : 8 + height, lanes] + st[b, stride * k + row0 : stride * k + row0 + height, :]


def kernel(
    T, NB, NS, stack, out,
    a0, x0, u0, w0, r0, a1, x1, u1, w1, r1, a2, x2, u2, w2, r2, a3, x3, u3, w3, r3, a4, x4, u4, w4,
    tiles, win, sent, got, rows_sent, rows_got,
    coef_own, coef_side, coef_pack, src_own, src_side, src_pack, side_rows,
    in_sem, halo_send, halo_recv, coef_send, coef_recv, src_send, src_recv, row_send, row_recv,
):
    turn = itertools.cycle(range(BUFFERS))

    def st():
        return tiles.at[next(turn)]

    t = lax.axis_index("tiles")
    col = lax.axis_index("band") * NS + lax.axis_index("stokes")
    cols = NB * NS
    h, w = stack.shape[1], stack.shape[2]
    has = {-1: col > 0, 0: None, 1: col < cols - 1}
    rowhas = {-1: t > 0, 0: None, 1: t < T - 1}

    def when(*conds):
        conds = [c for c in conds if c is not None]
        if not conds:
            return lambda f: f()
        return pl.when(functools.reduce(jnp.logical_and, conds))

    def device(tile, dc):
        c = col + dc
        return {"tiles": tile, "band": c // NS, "stokes": lax.rem(c, NS)}

    own_rows, own_cols = slice(HALO, HALO + h), slice(0, w)
    load = pltpu.make_async_copy(stack, a0.at[:, own_rows, own_cols], in_sem.at[0])
    load.start()

    partners = [(dt, dc) for dc in (-1, 0, 1) for dt in range(T) if dt or dc]
    barrier = pltpu.get_barrier_semaphore()
    for dt, dc in partners:
        @when(has[dc])
        def _(dt=dt, dc=dc):
            pl.semaphore_signal(barrier, inc=1, device_id=device(lax.rem(t + dt, T), dc), device_id_type=MESH)


    lane = iota((8, SIDE), 1)
    for q in range(h // 8):
        rows = slice(8 * q, 8 * q + 8)
        head = tail = jnp.zeros((8, SIDE), F32)
        for i in range(11):
            here = (lane >= DEEP * i) & (lane < DEEP * i + DEEP)
            one, two = stack[i, rows, 0:SIDE], stack[i, rows, w - SIDE : w]
            head = jnp.where(here, pltpu.roll(one, DEEP * i, 1) if i else one, head)
            tail = jnp.where(here, pltpu.roll(two, (DEEP * i + DEEP) % SIDE, 1), tail)
        sent[0, 8 * q : 8 * q + 8], sent[1, 8 * q : 8 * q + 8] = head, tail
    at = 0
    for i, n in enumerate(NEAR_ROWS):
        rows_sent[0, at : at + n] = stack[i, 0:n]
        rows_sent[1, at : at + n] = stack[i, h - n : h]
        at += n

    sides = 1 + jnp.where(col > 0, 1, 0) + jnp.where(col < cols - 1, 1, 0)
    pl.semaphore_wait(barrier, sides * T - 1)

    row_dst = {-1: slice(HALO + h, 2 * HALO + h), 0: own_rows, 1: slice(0, HALO)}
    part_src = {-1: slice(0, HALO), 0: slice(0, h), 1: slice(h - HALO, h)}

    def halo(dr, dc):
        i = (dr + 1) * 3 + dc + 1
        if dc:
            src = sent.at[(dc + 1) // 2, part_src[dr]]
            dst = got.at[(1 - dc) // 2, row_dst[dr]]
        else:
            src, dst = rows_sent.at[(dr + 1) // 2], rows_got.at[(1 - dr) // 2]
        return pltpu.make_async_remote_copy(
            src_ref=src,
            dst_ref=dst,
            send_sem=halo_send.at[i],
            recv_sem=halo_recv.at[i],
            device_id=device(t + dr, dc),
            device_id_type=MESH,
        )

    ways = [(0, -1), (0, 1), (-1, -1), (-1, 1), (1, -1), (1, 1), (-1, 0), (1, 0)]
    for dr, dc in ways:
        @when(rowhas[dr], has[dc])
        def _(dr=dr, dc=dc):
            halo(dr, dc).start()

    @pl.when(t == 0)
    def _():
        got[:, 0:HALO] = jnp.zeros_like(got[:, 0:HALO])
        side_rows[0] = jnp.zeros_like(side_rows[0])

    @pl.when(t == T - 1)
    def _():
        got[:, HALO + h :] = jnp.zeros_like(got[:, HALO + h :])
        side_rows[1] = jnp.zeros_like(side_rows[1])

    @pl.when(col == 0)
    def _():
        got[0] = jnp.zeros_like(got[0])
        coef_side[:, 0] = jnp.zeros_like(coef_side[:, 0])
        src_side[:, 0] = jnp.zeros_like(src_side[:, 0])

    @pl.when(col == cols - 1)
    def _():
        got[1] = jnp.zeros_like(got[1])
        coef_side[:, 1] = jnp.zeros_like(coef_side[:, 1])
        src_side[:, 1] = jnp.zeros_like(src_side[:, 1])

    a0[:, 0:HALO, own_cols] = jnp.zeros_like(a0[:, 0:HALO, own_cols])
    a0[:, HALO + h :, own_cols] = jnp.zeros_like(a0[:, HALO + h :, own_cols])
    for a in (a1, a3, a4):
        a[...] = jnp.zeros_like(a)
    for v in (x0, u0, x1, u1, x2, u2, x3, u3, x4, u4):
        v[:, 0:8, :] = jnp.zeros_like(v[:, 0:8, :])
        n = v.shape[1]
        v[:, n - 8 : n, :] = jnp.zeros_like(v[:, n - 8 : n, :])

    def gather(own, side, pack, send, recv, dt, dc):
        if dc:
            src, dst = pack.at[(dc + 1) // 2], side.at[t, (1 - dc) // 2]
        else:
            src, dst = own.at[t], own.at[t]
        return pltpu.make_async_remote_copy(
            src_ref=src,
            dst_ref=dst,
            send_sem=send.at[dt, dc + 1],
            recv_sem=recv.at[t, 1 - dc],
            device_id=device(lax.rem(t + dt, T), dc),
            device_id_type=MESH,
        )

    def arrival(own, side, pack, send, recv, dt, dc):
        s = lax.rem(t + dt, T)
        dst = side.at[s, (dc + 1) // 2] if dc else own.at[s]
        return pltpu.make_async_remote_copy(
            src_ref=dst,
            dst_ref=dst,
            send_sem=send.at[dt, dc + 1],
            recv_sem=recv.at[s, dc + 1],
            device_id=device(s, dc),
            device_id_type=MESH,
        )

    coef = (coef_own, coef_side, coef_pack, coef_send, coef_recv)
    src = (src_own, src_side, src_pack, src_send, src_recv)

    def scatter(x, way):
        own, pack = way[0], way[2]
        n = x.shape[0] // 2
        low = iota((n, SIDE), 1) < 64
        own[t] = x
        pack[0] = jnp.where(low, x[:n], pltpu.roll(x[n:], 64, 1))
        pack[1] = jnp.where(low, pltpu.roll(x[:n], 64, 1), x[n:])
        for dt, dc in partners:
            @when(has[dc])
            def _(dt=dt, dc=dc):
                gather(*way, dt, dc).start()

    def assemble(way, channel, count):
        for dt, dc in partners:
            @when(has[dc])
            def _(dt=dt, dc=dc):
                arrival(*way, dt, dc).wait_recv()
        own, side = way[:2]
        n = side.shape[2]
        low = iota((n, SIDE), 1) < 64

        def beside(s):
            left, right = side[s, 0], side[s, 1]
            return jnp.concatenate(
                [jnp.where(low, right, pltpu.roll(left, 64, 1)), jnp.where(low, pltpu.roll(right, 64, 1), left)], 0
            )

        for j in range(T // 2):
            for c in range(2):
                one, two = (beside(2 * j), beside(2 * j + 1)) if c else (own[2 * j], own[2 * j + 1])
                for i in range(count):
                    a2[channel + i, 8 * j : 8 * j + 8, SIDE * c : SIDE * c + SIDE] = jnp.concatenate(
                        [one[4 * i : 4 * i + 4], two[4 * i : 4 * i + 4]], 0
                    )

    even, odd = pool_matrix(256, 128), pool_matrix(256, 128, odd=True)
    even_ring, odd_ring = ring_pool(64), ring_pool(64, odd=True)
    wide = spread_matrix(128, 256)

    fine = [stack[3 + i] for i in range(8)]
    mid = coarsen_coefficients(fine, st, even, odd)
    for i in range(8):
        put(a1, 3 + i, 8, mid[i])
    mid = [jnp.concatenate(parts, 1) for parts in mid]
    low = [parts[0] for parts in coarsen_coefficients(mid, st, even, odd)]
    scatter(jnp.concatenate(low, 0), coef)

    for dr, dc in ways:
        if dc:
            @when(rowhas[dr], has[dc])
            def _(dr=dr, dc=dc):
                halo(-dr, -dc).wait_recv()

    for q in range(a0.shape[1] // 8):
        rows = slice(8 * q, 8 * q + 8)
        for i in range(11):
            right = pltpu.roll(got[1, rows], SIDE - DEEP * i, 1) if i else got[1, rows]
            left = pltpu.roll(got[0, rows], SIDE - DEEP - DEEP * i, 1)
            a0[i, rows, w : w + SIDE] = jnp.where(
                lane < DEEP, right, jnp.where(lane >= SIDE - DEEP, left, 0.0)
            )

    ends = [a0[3 + i, :, w : w + SIDE] for i in range(8)]
    for i, parts in enumerate(coarsen_coefficients(ends, st, even_ring, odd_ring)):
        put(a1, 3 + i, 4, parts, 2)

    for dr in (-1, 1):
        @when(rowhas[dr])
        def _(dr=dr):
            halo(-dr, 0).wait_recv()
            at = 0
            for i, n in enumerate(NEAR_ROWS):
                top = HALO - n if dr < 0 else HALO + h
                a0[i, top : top + n, own_cols] = rows_got[(dr + 1) // 2, at : at + n]
                at += n

    load.wait()

    setup(a0, w0)
    first(a0, w0, x0)
    sweep(a0, w0, x0, u0)
    residual(a0, w0, u0, r0)
    source = pool_rows(pool_lanes(r0[...], even, even_ring), st)
    h1 = a0.shape[1] // 2
    for k in range(3):
        put(a1, k, 4, [p[k * h1 : k * h1 + h1] for p in source])
    beside = [
        jnp.concatenate([a0[3 + i, 0:HALO, own_cols], a0[3 + i, HALO + h :, own_cols]], 0) for i in range(8)
    ]
    for i, parts in enumerate(coarsen_coefficients(beside, st, even, odd)):
        put(a1, 3 + i, 4, [p[:4] for p in parts])
        put(a1, 3 + i, 16, [p[4:] for p in parts])
    setup(a1, w1)
    first(a1, w1, x1)
    sweep(a1, w1, x1, u1)
    residual(a1, w1, u1, r1)
    own = dot(r1[:, 0:256], even)
    source = pool_rows([own], st)[0]
    packed = [source[12 * k + 4 : 12 * k + 8] for k in range(3)]
    scatter(jnp.concatenate(packed + [jnp.zeros((4, SIDE), F32)], 0), src)

    def rows_copy(dr):
        i = (dr + 1) // 2
        return pltpu.make_async_remote_copy(
            src_ref=u1.at[:, 16:24, :],
            dst_ref=side_rows.at[1 - i],
            send_sem=row_send.at[i],
            recv_sem=row_recv.at[1 - i],
            device_id=device(t + dr, 0),
            device_id_type=MESH,
        )

    for dr in (-1, 1):
        @when(rowhas[dr])
        def _(dr=dr):
            rows_copy(dr).start()

    assemble(coef, 3, 8)
    setup(a2, w2)
    last, last_odd = ring_pool(96), ring_pool(96, odd=True)
    for a, b, aux, p, p_odd in ((a2, a3, w3, even, odd), (a3, a4, w4, last, last_odd)):
        for i, parts in enumerate(coarsen_coefficients([a[3 + i] for i in range(8)], st, p, p_odd)):
            put(b, 3 + i, 0, parts)
        setup(b, aux)
    assemble(src, 0, 3)

    for a, aux, x, u, r, b, p in ((a2, w2, x2, u2, r2, a3, even), (a3, w3, x3, u3, r3, a4, last)):
        first(a, aux, x)
        sweep(a, aux, x, u)
        residual(a, aux, u, r)
        source = pool_rows(pool_lanes(r[...], p), st)
        n = a.shape[1] // 2
        for k in range(3):
            put(b, k, 0, [z[k * n : k * n + n] for z in source])
    if h // 16 * T < 8:
        n = [a4[3 + i] for i in range(6)]
        down, right, up, left, total = a4[9], a4[10], w4[0], w4[1], w4[2]
        source, scale = [a4[k] for k in range(3)], [w4[3 + k] for k in range(3)]
        v = [scale[k] * source[k] for k in range(3)]
        weight = [n[k] + total for k in range(3)]
        for _ in range(COARSE_SWEEPS - 1):
            cross = [n[3] * v[1] + n[4] * v[2], n[3] * v[0] + n[5] * v[2], n[4] * v[0] + n[5] * v[1]]
            new = []
            for k in range(3):
                near = (down * pltpu.roll(v[k], 7, 0) + up * pltpu.roll(v[k], 1, 0)) + (
                    right * pltpu.roll(v[k], SIDE - 1, 1) + left * pltpu.roll(v[k], 1, 1)
                )
                new.append(v[k] + scale[k] * (source[k] - (weight[k] * v[k] + cross[k]) + near))
            v = new
    else:
        first(a4, w4, x4)
        now, then = x4, u4
        for _ in range(COARSE_SWEEPS - 1):
            sweep(a4, w4, now, then)
            now, then = then, now
        v = [now[k, 8 : 8 + a4.shape[1]] for k in range(3)]
    for a, aux, x, u in ((a3, w3, x3, u3), (a2, w2, x2, u2)):
        n = v[0].shape[0]
        z = dot(jnp.concatenate(v, 0), wide if a is a2 else ring_spread(SIDE, SIDE, 96))
        parts = [z[:, b : b + SIDE] for b in range(0, z.shape[1], SIDE)]
        add_spread(u, x, spread_rows(parts, st), 2 * n, len(parts), a.shape[1])
        sweep(a, aux, x, u)
        sweep(a, aux, u, x)
        v = [x[k, 8 : 8 + a.shape[1]] for k in range(3)]

    for s in range(T):
        @pl.when(t == s)
        def _(s=s):
            for k in range(3):
                win[16 * k : 16 * k + 16, :] = x2[k, 4 + 4 * s : 20 + 4 * s]
    y = dot(win[...], ring_spread(256, 384, 320))
    spread = spread_rows([y[:, 128 * b : 128 * b + 128] for b in range(3)], st)
    for dr in (-1, 1):
        @when(rowhas[dr])
        def _(dr=dr):
            rows_copy(dr).wait_send()
            rows_copy(-dr).wait_recv()
    u1[:, 8:16, :] = side_rows[0]
    u1[:, 24:32, :] = side_rows[1]
    add_spread(u1, x1, spread, 32, 3, 24)
    sweep(a1, w1, x1, u1)
    sweep(a1, w1, u1, x1)

    y = jnp.concatenate([x1[k, 8:32] for k in range(3)], 0)
    parts = []
    for b in range(2):
        z = dot(y[:, 128 * b : 128 * b + 128], wide)
        parts += [z[:, :128], z[:, 128:]]
    parts.append(dot(y[:, 256:384], ring_spread(SIDE, SIDE, 64)))
    add_spread(u0, x0, spread_rows(parts, st), 48, 5, 32, row0=8)
    sweep(a0, w0, x0, u0)
    for q in range(1, 1 + h // 8):
        mid, res = residual_at(a0, w0, u0, q)
        for k in range(3):
            new = mid[k] + w0[3 + k, 8 * q : 8 * q + 8] * res[k]
            out[k, 8 * q - 8 : 8 * q, :] = new[:, own_cols]

    for dr, dc in ways:
        @when(rowhas[dr], has[dc])
        def _(dr=dr, dc=dc):
            halo(dr, dc).wait_send()
    for dt, dc in partners:
        @when(has[dc])
        def _(dt=dt, dc=dc):
            gather(*coef, dt, dc).wait_send()
            gather(*src, dt, dc).wait_send()


def on_device(right_side, noise_block, edges):
    T, NB, NS = lax.axis_size("tiles"), lax.axis_size("band"), lax.axis_size("stokes")
    _, h, w = right_side.shape
    shapes = [
        (h + 2 * HALO, w + SIDE),
        (h // 2 + 16, w // 2 + SIDE),
        (h // 4 * T, 2 * SIDE),
        (max(8, h // 8 * T), SIDE),
        (max(8, h // 16 * T), SIDE),
    ]
    scratch = []
    for i, (n, m) in enumerate(shapes):
        scratch += [
            pltpu.VMEM((11, n, m), F32),
            pltpu.VMEM((3, n + 16, m), F32),
            pltpu.VMEM((3, n + 16, m), F32),
            pltpu.VMEM((6, n, m), F32),
        ]
        if i < 4:
            scratch.append(pltpu.VMEM((3 * n, m), F32))
    scratch += [
        pltpu.VMEM((BUFFERS, 5, max(6 * 32, 6 * h // 4 * T), SIDE), F32),
        pltpu.VMEM((48, 2 * SIDE), F32),
        pltpu.VMEM((2, h, SIDE), F32),
        pltpu.VMEM((2, h + 2 * HALO, SIDE), F32),
        pltpu.VMEM((2, sum(NEAR_ROWS), w), F32),
        pltpu.VMEM((2, sum(NEAR_ROWS), w), F32),
        pltpu.VMEM((T, 32, SIDE), F32),
        pltpu.VMEM((T, 2, 16, SIDE), F32),
        pltpu.VMEM((2, 16, SIDE), F32),
        pltpu.VMEM((T, 16, SIDE), F32),
        pltpu.VMEM((T, 2, 8, SIDE), F32),
        pltpu.VMEM((2, 8, SIDE), F32),
        pltpu.VMEM((2, 3, 8, 3 * SIDE), F32),
        pltpu.SemaphoreType.DMA((1,)),
        pltpu.SemaphoreType.DMA((9,)),
        pltpu.SemaphoreType.DMA((9,)),
        pltpu.SemaphoreType.DMA((T, 3)),
        pltpu.SemaphoreType.DMA((T, 3)),
        pltpu.SemaphoreType.DMA((T, 3)),
        pltpu.SemaphoreType.DMA((T, 3)),
        pltpu.SemaphoreType.DMA((2,)),
        pltpu.SemaphoreType.DMA((2,)),
    ]
    return pl.pallas_call(
        functools.partial(kernel, T, NB, NS),
        out_shape=jax.ShapeDtypeStruct(right_side.shape, F32),
        in_specs=[pl.BlockSpec(memory_space=pltpu.VMEM)],
        out_specs=pl.BlockSpec(memory_space=pltpu.VMEM),
        scratch_shapes=scratch,
        compiler_params=pltpu.CompilerParams(
            collective_id=0, has_side_effects=True, vmem_limit_bytes=40 * 1024 * 1024
        ),
    )(jnp.concatenate([right_side, noise_block, edges], 0))


def solution(mesh):
    spec = P(None, ("groups", "tiles"), ("band", "stokes"))
    return jax.shard_map(
        on_device, mesh=mesh, in_specs=(spec, spec, spec), out_specs=spec, check_vma=False
    )
```

```python
import functools
import itertools

import jax
import jax.numpy as jnp
from jax import lax
from jax.experimental import pallas as pl
from jax.experimental.pallas import tpu as pltpu
from jax.sharding import PartitionSpec as P

OMEGA = 0.8
COARSE_SWEEPS = 8
HALO = 8
SIDE = 128
DEEP = 11
BUFFERS = 12
NEAR_ROWS = (6, 6, 6, 6, 6, 6, 5, 5, 5, 7, 6)
MESH = pl.DeviceIdType.MESH
F32 = jnp.float32


def rounded(x):
    return x.astype(jnp.bfloat16).astype(F32)


def dot(x, y):
    n = x.shape[0]
    high = rounded(x)
    pieces = jnp.concatenate([high, x - high], 0)
    z = jnp.dot(pieces, y, precision=lax.Precision.DEFAULT, preferred_element_type=F32)
    return z[:n] + z[n:]


def iota(shape, dim):
    return lax.broadcasted_iota(jnp.int32, shape, dim)


def ones(hit):
    return jnp.where(hit, 1.0, 0.0).astype(F32)


def half(i):
    return lax.shift_right_logical(i, 1)


def pool_matrix(n, m, odd=False):
    c, j = iota((n, m), 0), iota((n, m), 1)
    hit = c == 2 * j + 1
    return ones(hit if odd else hit | (c == 2 * j))


def spread_matrix(n, m):
    c, j = iota((n, m), 0), iota((n, m), 1)
    return ones(c == half(j))


def ring_pool(cut, odd=False):
    c, j = iota((SIDE, SIDE), 0), iota((SIDE, SIDE), 1)
    hit = j == half(c) + jnp.where(c >= cut, 64, 0)
    return ones(hit & ((c & 1) == 1) if odd else hit)


def ring_spread(n, m, cut):
    c, j = iota((n, m), 0), iota((n, m), 1)
    return ones(c == half(j) + jnp.where(j >= cut, 64, 0))


def chunks(a):
    return range(a.shape[1] // 8)


def setup(a, aux):
    for q in chunks(a):
        rows = slice(8 * q, 8 * q + 8)
        down, right = a[9, rows], a[10, rows]
        if q == 0:
            up = jnp.where(iota(down.shape, 0) == 0, 0.0, pltpu.roll(down, 1, 0))
        else:
            up = a[9, 8 * q - 1 : 8 * q + 7]
        left = pltpu.roll(right, 1, 1)
        total = down + up + right + left
        aux[0, rows], aux[1, rows], aux[2, rows] = up, left, total
        for k in range(3):
            aux[3 + k, rows] = jnp.where(down > 0, OMEGA / (a[3 + k, rows] + total), 0.0)


def first(a, aux, v):
    for q in chunks(a):
        rows = slice(8 * q, 8 * q + 8)
        for k in range(3):
            v[k, 8 + 8 * q : 16 + 8 * q] = aux[3 + k, rows] * a[k, rows]


def residual_at(a, aux, v, q):
    rows = slice(8 * q, 8 * q + 8)
    mid = [v[k, 8 + 8 * q : 16 + 8 * q] for k in range(3)]
    n = [a[3 + i, rows] for i in range(6)]
    down, right, up, left, total = a[9, rows], a[10, rows], aux[0, rows], aux[1, rows], aux[2, rows]
    width = mid[0].shape[1]
    image = [
        n[0] * mid[0] + n[3] * mid[1] + n[4] * mid[2],
        n[3] * mid[0] + n[1] * mid[1] + n[5] * mid[2],
        n[4] * mid[0] + n[5] * mid[1] + n[2] * mid[2],
    ]
    out = []
    for k in range(3):
        near = (
            down * v[k, 9 + 8 * q : 17 + 8 * q]
            + up * v[k, 7 + 8 * q : 15 + 8 * q]
            + right * pltpu.roll(mid[k], width - 1, 1)
            + left * pltpu.roll(mid[k], 1, 1)
        )
        out.append(a[k, rows] - (image[k] + total * mid[k] - near))
    return mid, out


def sweep(a, aux, src, dst, which=None):
    for q in chunks(a) if which is None else which:
        mid, res = residual_at(a, aux, src, q)
        for k in range(3):
            dst[k, 8 + 8 * q : 16 + 8 * q] = mid[k] + aux[3 + k, 8 * q : 8 * q + 8] * res[k]


def residual(a, aux, v, r):
    height = a.shape[1]
    for q in chunks(a):
        _, res = residual_at(a, aux, v, q)
        for k in range(3):
            r[k * height + 8 * q : k * height + 8 * q + 8, :] = res[k]


def pool_lanes(x, matrix, tail=None):
    n = matrix.shape[0]
    width = x.shape[1]
    parts = []
    for b in range(0, width, n):
        if b + n <= width:
            parts.append(dot(x[:, b : b + n], matrix))
        else:
            parts.append(dot(x[:, b:width], matrix[: width - b] if tail is None else tail))
    return parts


def pool_rows(parts, st, odd=False):
    st = st()
    out = []
    for b, part in enumerate(parts):
        n = part.shape[0]
        st[b, 0:n, :] = part
        top = st[b, pl.ds(1, n // 2, stride=2), :]
        out.append(top if odd else top + st[b, pl.ds(0, n // 2, stride=2), :])
    return out


def coarsen_coefficients(arrays, st, even, odd):
    h = arrays[0].shape[0]
    parts = pool_lanes(jnp.concatenate(arrays[:7], 0), even)
    noise = pool_rows([p[: 6 * h] for p in parts], st)
    down = pool_rows([p[6 * h :] for p in parts], st, odd=True)
    right = pool_rows(pool_lanes(arrays[7], odd), st)
    h = h // 2
    out = []
    for i in range(6):
        out.append([p[i * h : i * h + h] for p in noise])
    return out + [down, right]


def spread_rows(parts, st):
    st = st()
    for b, part in enumerate(parts):
        n = part.shape[0]
        st[b, pl.ds(0, n, stride=2), :] = part
        st[b, pl.ds(1, n, stride=2), :] = part
    return st


def put(a, channel, row, parts, tile=0):
    for b, part in enumerate(parts, tile):
        a[channel, row : row + part.shape[0], SIDE * b : SIDE * b + SIDE] = part


def add_spread(v, dst, st, stride, blocks, height, row0=0):
    for k in range(3):
        for b in range(blocks):
            lanes = slice(SIDE * b, SIDE * b + SIDE)
            dst[k, 8 : 8 + height, lanes] = v[k, 8 : 8 + height, lanes] + st[b, stride * k + row0 : stride * k + row0 + height, :]


def kernel(
    T, NB, NS, stack, out,
    a0, x0, u0, w0, r0, a1, x1, u1, w1, r1, a2, x2, u2, w2, r2, a3, x3, u3, w3, r3, a4, x4, u4, w4,
    tiles, win, sent, got, rows_sent, rows_got,
    coef_own, coef_side, coef_pack, src_own, src_side, src_pack, side_rows,
    in_sem, halo_send, halo_recv, coef_send, coef_recv, src_send, src_recv, row_send, row_recv,
):
    turn = itertools.cycle(range(BUFFERS))

    def st():
        return tiles.at[next(turn)]

    t = lax.axis_index("tiles")
    col = lax.axis_index("band") * NS + lax.axis_index("stokes")
    cols = NB * NS
    h, w = stack.shape[1], stack.shape[2]
    has = {-1: col > 0, 0: None, 1: col < cols - 1}
    rowhas = {-1: t > 0, 0: None, 1: t < T - 1}

    def when(*conds):
        conds = [c for c in conds if c is not None]
        if not conds:
            return lambda f: f()
        return pl.when(functools.reduce(jnp.logical_and, conds))

    def device(tile, dc):
        c = col + dc
        return {"tiles": tile, "band": c // NS, "stokes": lax.rem(c, NS)}

    own_rows, own_cols = slice(HALO, HALO + h), slice(0, w)
    load = pltpu.make_async_copy(stack, a0.at[:, own_rows, own_cols], in_sem.at[0])
    load.start()

    partners = [(dt, dc) for dc in (-1, 0, 1) for dt in range(T) if dt or dc]
    barrier = pltpu.get_barrier_semaphore()
    for dt, dc in partners:
        @when(has[dc])
        def _(dt=dt, dc=dc):
            pl.semaphore_signal(barrier, inc=1, device_id=device(lax.rem(t + dt, T), dc), device_id_type=MESH)


    lane = iota((8, SIDE), 1)
    for q in range(h // 8):
        rows = slice(8 * q, 8 * q + 8)
        head = tail = jnp.zeros((8, SIDE), F32)
        for i in range(11):
            here = (lane >= DEEP * i) & (lane < DEEP * i + DEEP)
            one, two = stack[i, rows, 0:SIDE], stack[i, rows, w - SIDE : w]
            head = jnp.where(here, pltpu.roll(one, DEEP * i, 1) if i else one, head)
            tail = jnp.where(here, pltpu.roll(two, (DEEP * i + DEEP) % SIDE, 1), tail)
        sent[0, 8 * q : 8 * q + 8], sent[1, 8 * q : 8 * q + 8] = head, tail
    at = 0
    for i, n in enumerate(NEAR_ROWS):
        rows_sent[0, at : at + n] = stack[i, 0:n]
        rows_sent[1, at : at + n] = stack[i, h - n : h]
        at += n

    sides = 1 + jnp.where(col > 0, 1, 0) + jnp.where(col < cols - 1, 1, 0)
    pl.semaphore_wait(barrier, sides * T - 1)

    row_dst = {-1: slice(HALO + h, 2 * HALO + h), 0: own_rows, 1: slice(0, HALO)}
    part_src = {-1: slice(0, HALO), 0: slice(0, h), 1: slice(h - HALO, h)}

    def halo(dr, dc):
        i = (dr + 1) * 3 + dc + 1
        if dc:
            src = sent.at[(dc + 1) // 2, part_src[dr]]
            dst = got.at[(1 - dc) // 2, row_dst[dr]]
        else:
            src, dst = rows_sent.at[(dr + 1) // 2], rows_got.at[(1 - dr) // 2]
        return pltpu.make_async_remote_copy(
            src_ref=src,
            dst_ref=dst,
            send_sem=halo_send.at[i],
            recv_sem=halo_recv.at[i],
            device_id=device(t + dr, dc),
            device_id_type=MESH,
        )

    ways = [(0, -1), (0, 1), (-1, -1), (-1, 1), (1, -1), (1, 1), (-1, 0), (1, 0)]
    for dr, dc in ways:
        @when(rowhas[dr], has[dc])
        def _(dr=dr, dc=dc):
            halo(dr, dc).start()

    @pl.when(t == 0)
    def _():
        got[:, 0:HALO] = jnp.zeros_like(got[:, 0:HALO])
        side_rows[0] = jnp.zeros_like(side_rows[0])

    @pl.when(t == T - 1)
    def _():
        got[:, HALO + h :] = jnp.zeros_like(got[:, HALO + h :])
        side_rows[1] = jnp.zeros_like(side_rows[1])

    @pl.when(col == 0)
    def _():
        got[0] = jnp.zeros_like(got[0])
        coef_side[:, 0] = jnp.zeros_like(coef_side[:, 0])
        src_side[:, 0] = jnp.zeros_like(src_side[:, 0])

    @pl.when(col == cols - 1)
    def _():
        got[1] = jnp.zeros_like(got[1])
        coef_side[:, 1] = jnp.zeros_like(coef_side[:, 1])
        src_side[:, 1] = jnp.zeros_like(src_side[:, 1])

    a0[:, 0:HALO, own_cols] = jnp.zeros_like(a0[:, 0:HALO, own_cols])
    a0[:, HALO + h :, own_cols] = jnp.zeros_like(a0[:, HALO + h :, own_cols])
    for a in (a1, a3, a4):
        a[...] = jnp.zeros_like(a)
    for v in (x0, u0, x1, u1, x2, u2, x3, u3, x4, u4):
        v[:, 0:8, :] = jnp.zeros_like(v[:, 0:8, :])
        n = v.shape[1]
        v[:, n - 8 : n, :] = jnp.zeros_like(v[:, n - 8 : n, :])

    def gather(own, side, pack, send, recv, dt, dc):
        if dc:
            src, dst = pack.at[(dc + 1) // 2], side.at[t, (1 - dc) // 2]
        else:
            src, dst = own.at[t], own.at[t]
        return pltpu.make_async_remote_copy(
            src_ref=src,
            dst_ref=dst,
            send_sem=send.at[dt, dc + 1],
            recv_sem=recv.at[t, 1 - dc],
            device_id=device(lax.rem(t + dt, T), dc),
            device_id_type=MESH,
        )

    def arrival(own, side, pack, send, recv, dt, dc):
        s = lax.rem(t + dt, T)
        dst = side.at[s, (dc + 1) // 2] if dc else own.at[s]
        return pltpu.make_async_remote_copy(
            src_ref=dst,
            dst_ref=dst,
            send_sem=send.at[dt, dc + 1],
            recv_sem=recv.at[s, dc + 1],
            device_id=device(s, dc),
            device_id_type=MESH,
        )

    coef = (coef_own, coef_side, coef_pack, coef_send, coef_recv)
    src = (src_own, src_side, src_pack, src_send, src_recv)

    def scatter(x, way):
        own, pack = way[0], way[2]
        n = x.shape[0] // 2
        low = iota((n, SIDE), 1) < 64
        own[t] = x
        pack[0] = jnp.where(low, x[:n], pltpu.roll(x[n:], 64, 1))
        pack[1] = jnp.where(low, pltpu.roll(x[:n], 64, 1), x[n:])
        for dt, dc in partners:
            @when(has[dc])
            def _(dt=dt, dc=dc):
                gather(*way, dt, dc).start()

    def assemble(way, channel, count):
        for dt, dc in partners:
            @when(has[dc])
            def _(dt=dt, dc=dc):
                arrival(*way, dt, dc).wait_recv()
        own, side = way[:2]
        n = side.shape[2]
        low = iota((n, SIDE), 1) < 64

        def beside(s):
            left, right = side[s, 0], side[s, 1]
            return jnp.concatenate(
                [jnp.where(low, right, pltpu.roll(left, 64, 1)), jnp.where(low, pltpu.roll(right, 64, 1), left)], 0
            )

        for j in range(T // 2):
            for c in range(2):
                one, two = (beside(2 * j), beside(2 * j + 1)) if c else (own[2 * j], own[2 * j + 1])
                for i in range(count):
                    a2[channel + i, 8 * j : 8 * j + 8, SIDE * c : SIDE * c + SIDE] = jnp.concatenate(
                        [one[4 * i : 4 * i + 4], two[4 * i : 4 * i + 4]], 0
                    )

    even, odd = pool_matrix(256, 128), pool_matrix(256, 128, odd=True)
    even_ring, odd_ring = ring_pool(64), ring_pool(64, odd=True)
    wide = spread_matrix(128, 256)

    fine = [stack[3 + i] for i in range(8)]
    mid = coarsen_coefficients(fine, st, even, odd)
    for i in range(8):
        put(a1, 3 + i, 8, mid[i])
    mid = [jnp.concatenate(parts, 1) for parts in mid]
    low = [parts[0] for parts in coarsen_coefficients(mid, st, even, odd)]
    scatter(jnp.concatenate(low, 0), coef)

    for dr, dc in ways:
        if dc:
            @when(rowhas[dr], has[dc])
            def _(dr=dr, dc=dc):
                halo(-dr, -dc).wait_recv()

    for q in range(a0.shape[1] // 8):
        rows = slice(8 * q, 8 * q + 8)
        for i in range(11):
            right = pltpu.roll(got[1, rows], SIDE - DEEP * i, 1) if i else got[1, rows]
            left = pltpu.roll(got[0, rows], SIDE - DEEP - DEEP * i, 1)
            a0[i, rows, w : w + SIDE] = jnp.where(
                lane < DEEP, right, jnp.where(lane >= SIDE - DEEP, left, 0.0)
            )

    ends = [a0[3 + i, :, w : w + SIDE] for i in range(8)]
    for i, parts in enumerate(coarsen_coefficients(ends, st, even_ring, odd_ring)):
        put(a1, 3 + i, 4, parts, 2)

    for dr in (-1, 1):
        @when(rowhas[dr])
        def _(dr=dr):
            halo(-dr, 0).wait_recv()
            at = 0
            for i, n in enumerate(NEAR_ROWS):
                top = HALO - n if dr < 0 else HALO + h
                a0[i, top : top + n, own_cols] = rows_got[(dr + 1) // 2, at : at + n]
                at += n

    load.wait()

    beside = [
        jnp.concatenate([a0[3 + i, 0:HALO, own_cols], a0[3 + i, HALO + h :, own_cols]], 0) for i in range(8)
    ]
    for i, parts in enumerate(coarsen_coefficients(beside, st, even, odd)):
        put(a1, 3 + i, 4, [p[:4] for p in parts])
        put(a1, 3 + i, 16, [p[4:] for p in parts])
    setup(a1, w1)

    setup(a0, w0)
    first(a0, w0, x0)
    sweep(a0, w0, x0, u0)
    residual(a0, w0, u0, r0)
    source = pool_rows(pool_lanes(r0[...], even, even_ring), st)
    h1 = a0.shape[1] // 2
    for k in range(3):
        put(a1, k, 4, [p[k * h1 : k * h1 + h1] for p in source])
    first(a1, w1, x1)
    sweep(a1, w1, x1, u1)
    residual(a1, w1, u1, r1)
    own = dot(r1[:, 0:256], even)
    source = pool_rows([own], st)[0]
    packed = [source[12 * k + 4 : 12 * k + 8] for k in range(3)]
    scatter(jnp.concatenate(packed + [jnp.zeros((4, SIDE), F32)], 0), src)

    def rows_copy(dr):
        i = (dr + 1) // 2
        return pltpu.make_async_remote_copy(
            src_ref=u1.at[:, 16:24, :],
            dst_ref=side_rows.at[1 - i],
            send_sem=row_send.at[i],
            recv_sem=row_recv.at[1 - i],
            device_id=device(t + dr, 0),
            device_id_type=MESH,
        )

    for dr in (-1, 1):
        @when(rowhas[dr])
        def _(dr=dr):
            rows_copy(dr).start()

    assemble(coef, 3, 8)
    setup(a2, w2)
    last, last_odd = ring_pool(96), ring_pool(96, odd=True)
    for a, b, aux, p, p_odd in ((a2, a3, w3, even, odd), (a3, a4, w4, last, last_odd)):
        for i, parts in enumerate(coarsen_coefficients([a[3 + i] for i in range(8)], st, p, p_odd)):
            put(b, 3 + i, 0, parts)
        setup(b, aux)
    assemble(src, 0, 3)

    for a, aux, x, u, r, b, p in ((a2, w2, x2, u2, r2, a3, even), (a3, w3, x3, u3, r3, a4, last)):
        first(a, aux, x)
        sweep(a, aux, x, u)
        residual(a, aux, u, r)
        source = pool_rows(pool_lanes(r[...], p), st)
        n = a.shape[1] // 2
        for k in range(3):
            put(b, k, 0, [z[k * n : k * n + n] for z in source])
    if h // 16 * T < 8:
        n = [a4[3 + i] for i in range(6)]
        down, right, up, left, total = a4[9], a4[10], w4[0], w4[1], w4[2]
        source, scale = [a4[k] for k in range(3)], [w4[3 + k] for k in range(3)]
        v = [scale[k] * source[k] for k in range(3)]
        weight = [n[k] + total for k in range(3)]
        for _ in range(COARSE_SWEEPS - 1):
            cross = [n[3] * v[1] + n[4] * v[2], n[3] * v[0] + n[5] * v[2], n[4] * v[0] + n[5] * v[1]]
            new = []
            for k in range(3):
                near = (down * pltpu.roll(v[k], 7, 0) + up * pltpu.roll(v[k], 1, 0)) + (
                    right * pltpu.roll(v[k], SIDE - 1, 1) + left * pltpu.roll(v[k], 1, 1)
                )
                new.append(v[k] + scale[k] * (source[k] - (weight[k] * v[k] + cross[k]) + near))
            v = new
    else:
        first(a4, w4, x4)
        now, then = x4, u4
        for _ in range(COARSE_SWEEPS - 1):
            sweep(a4, w4, now, then)
            now, then = then, now
        v = [now[k, 8 : 8 + a4.shape[1]] for k in range(3)]
    for a, aux, x, u in ((a3, w3, x3, u3), (a2, w2, x2, u2)):
        n = v[0].shape[0]
        z = dot(jnp.concatenate(v, 0), wide if a is a2 else ring_spread(SIDE, SIDE, 96))
        parts = [z[:, b : b + SIDE] for b in range(0, z.shape[1], SIDE)]
        add_spread(u, x, spread_rows(parts, st), 2 * n, len(parts), a.shape[1])
        sweep(a, aux, x, u)
        sweep(a, aux, u, x)
        v = [x[k, 8 : 8 + a.shape[1]] for k in range(3)]

    for s in range(T):
        @pl.when(t == s)
        def _(s=s):
            for k in range(3):
                win[16 * k : 16 * k + 16, :] = x2[k, 4 + 4 * s : 20 + 4 * s]
    y = dot(win[...], ring_spread(256, 384, 320))
    spread = spread_rows([y[:, 128 * b : 128 * b + 128] for b in range(3)], st)
    for dr in (-1, 1):
        @when(rowhas[dr])
        def _(dr=dr):
            rows_copy(dr).wait_send()
            rows_copy(-dr).wait_recv()
    u1[:, 8:16, :] = side_rows[0]
    u1[:, 24:32, :] = side_rows[1]
    add_spread(u1, x1, spread, 32, 3, 24)
    sweep(a1, w1, x1, u1)
    sweep(a1, w1, u1, x1)

    y = jnp.concatenate([x1[k, 8:32] for k in range(3)], 0)
    parts = []
    for b in range(2):
        z = dot(y[:, 128 * b : 128 * b + 128], wide)
        parts += [z[:, :128], z[:, 128:]]
    parts.append(dot(y[:, 256:384], ring_spread(SIDE, SIDE, 64)))
    add_spread(u0, x0, spread_rows(parts, st), 48, 5, 32, row0=8)
    sweep(a0, w0, x0, u0)
    for q in range(1, 1 + h // 8):
        mid, res = residual_at(a0, w0, u0, q)
        for k in range(3):
            new = mid[k] + w0[3 + k, 8 * q : 8 * q + 8] * res[k]
            out[k, 8 * q - 8 : 8 * q, :] = new[:, own_cols]

    for dr, dc in ways:
        @when(rowhas[dr], has[dc])
        def _(dr=dr, dc=dc):
            halo(dr, dc).wait_send()
    for dt, dc in partners:
        @when(has[dc])
        def _(dt=dt, dc=dc):
            gather(*coef, dt, dc).wait_send()
            gather(*src, dt, dc).wait_send()


def on_device(right_side, noise_block, edges):
    T, NB, NS = lax.axis_size("tiles"), lax.axis_size("band"), lax.axis_size("stokes")
    _, h, w = right_side.shape
    shapes = [
        (h + 2 * HALO, w + SIDE),
        (h // 2 + 16, w // 2 + SIDE),
        (h // 4 * T, 2 * SIDE),
        (max(8, h // 8 * T), SIDE),
        (max(8, h // 16 * T), SIDE),
    ]
    scratch = []
    for i, (n, m) in enumerate(shapes):
        scratch += [
            pltpu.VMEM((11, n, m), F32),
            pltpu.VMEM((3, n + 16, m), F32),
            pltpu.VMEM((3, n + 16, m), F32),
            pltpu.VMEM((6, n, m), F32),
        ]
        if i < 4:
            scratch.append(pltpu.VMEM((3 * n, m), F32))
    scratch += [
        pltpu.VMEM((BUFFERS, 5, max(6 * 32, 6 * h // 4 * T), SIDE), F32),
        pltpu.VMEM((48, 2 * SIDE), F32),
        pltpu.VMEM((2, h, SIDE), F32),
        pltpu.VMEM((2, h + 2 * HALO, SIDE), F32),
        pltpu.VMEM((2, sum(NEAR_ROWS), w), F32),
        pltpu.VMEM((2, sum(NEAR_ROWS), w), F32),
        pltpu.VMEM((T, 32, SIDE), F32),
        pltpu.VMEM((T, 2, 16, SIDE), F32),
        pltpu.VMEM((2, 16, SIDE), F32),
        pltpu.VMEM((T, 16, SIDE), F32),
        pltpu.VMEM((T, 2, 8, SIDE), F32),
        pltpu.VMEM((2, 8, SIDE), F32),
        pltpu.VMEM((2, 3, 8, 3 * SIDE), F32),
        pltpu.SemaphoreType.DMA((1,)),
        pltpu.SemaphoreType.DMA((9,)),
        pltpu.SemaphoreType.DMA((9,)),
        pltpu.SemaphoreType.DMA((T, 3)),
        pltpu.SemaphoreType.DMA((T, 3)),
        pltpu.SemaphoreType.DMA((T, 3)),
        pltpu.SemaphoreType.DMA((T, 3)),
        pltpu.SemaphoreType.DMA((2,)),
        pltpu.SemaphoreType.DMA((2,)),
    ]
    return pl.pallas_call(
        functools.partial(kernel, T, NB, NS),
        out_shape=jax.ShapeDtypeStruct(right_side.shape, F32),
        in_specs=[pl.BlockSpec(memory_space=pltpu.VMEM)],
        out_specs=pl.BlockSpec(memory_space=pltpu.VMEM),
        scratch_shapes=scratch,
        compiler_params=pltpu.CompilerParams(
            collective_id=0, has_side_effects=True, vmem_limit_bytes=40 * 1024 * 1024
        ),
    )(jnp.concatenate([right_side, noise_block, edges], 0))


def solution(mesh):
    spec = P(None, ("groups", "tiles"), ("band", "stokes"))
    return jax.shard_map(
        on_device, mesh=mesh, in_specs=(spec, spec, spec), out_specs=spec, check_vma=False
    )
```

```python
import functools
import itertools

import jax
import jax.numpy as jnp
from jax import lax
from jax.experimental import pallas as pl
from jax.experimental.pallas import tpu as pltpu
from jax.sharding import PartitionSpec as P

OMEGA = 0.8
COARSE_SWEEPS = 8
HALO = 8
SIDE = 128
DEEP = 11
BUFFERS = 12
NEAR_ROWS = (6, 6, 6, 6, 6, 6, 5, 5, 5, 7, 6)
MESH = pl.DeviceIdType.MESH
F32 = jnp.float32


def rounded(x):
    return x.astype(jnp.bfloat16).astype(F32)


def dot(x, y):
    n = x.shape[0]
    high = rounded(x)
    pieces = jnp.concatenate([high, x - high], 0)
    z = jnp.dot(pieces, y, precision=lax.Precision.DEFAULT, preferred_element_type=F32)
    return z[:n] + z[n:]


def iota(shape, dim):
    return lax.broadcasted_iota(jnp.int32, shape, dim)


def ones(hit):
    return jnp.where(hit, 1.0, 0.0).astype(F32)


def half(i):
    return lax.shift_right_logical(i, 1)


def pool_matrix(n, m, odd=False):
    c, j = iota((n, m), 0), iota((n, m), 1)
    hit = c == 2 * j + 1
    return ones(hit if odd else hit | (c == 2 * j))


def spread_matrix(n, m):
    c, j = iota((n, m), 0), iota((n, m), 1)
    return ones(c == half(j))


def ring_pool(cut, odd=False):
    c, j = iota((SIDE, SIDE), 0), iota((SIDE, SIDE), 1)
    hit = j == half(c) + jnp.where(c >= cut, 64, 0)
    return ones(hit & ((c & 1) == 1) if odd else hit)


def ring_spread(n, m, cut):
    c, j = iota((n, m), 0), iota((n, m), 1)
    return ones(c == half(j) + jnp.where(j >= cut, 64, 0))


def chunks(a):
    return range(a.shape[1] // 8)


def setup(a, aux):
    for q in chunks(a):
        rows = slice(8 * q, 8 * q + 8)
        down, right = a[9, rows], a[10, rows]
        if q == 0:
            up = jnp.where(iota(down.shape, 0) == 0, 0.0, pltpu.roll(down, 1, 0))
        else:
            up = a[9, 8 * q - 1 : 8 * q + 7]
        left = pltpu.roll(right, 1, 1)
        total = down + up + right + left
        aux[0, rows], aux[1, rows], aux[2, rows] = up, left, total
        for k in range(3):
            aux[3 + k, rows] = jnp.where(down > 0, OMEGA / (a[3 + k, rows] + total), 0.0)


def first(a, aux, v):
    for q in chunks(a):
        rows = slice(8 * q, 8 * q + 8)
        for k in range(3):
            v[k, 8 + 8 * q : 16 + 8 * q] = aux[3 + k, rows] * a[k, rows]


def residual_at(a, aux, v, q):
    rows = slice(8 * q, 8 * q + 8)
    mid = [v[k, 8 + 8 * q : 16 + 8 * q] for k in range(3)]
    n = [a[3 + i, rows] for i in range(6)]
    down, right, up, left, total = a[9, rows], a[10, rows], aux[0, rows], aux[1, rows], aux[2, rows]
    width = mid[0].shape[1]
    image = [
        n[0] * mid[0] + n[3] * mid[1] + n[4] * mid[2],
        n[3] * mid[0] + n[1] * mid[1] + n[5] * mid[2],
        n[4] * mid[0] + n[5] * mid[1] + n[2] * mid[2],
    ]
    out = []
    for k in range(3):
        near = (
            down * v[k, 9 + 8 * q : 17 + 8 * q]
            + up * v[k, 7 + 8 * q : 15 + 8 * q]
            + right * pltpu.roll(mid[k], width - 1, 1)
            + left * pltpu.roll(mid[k], 1, 1)
        )
        out.append(a[k, rows] - (image[k] + total * mid[k] - near))
    return mid, out


def sweep(a, aux, src, dst, which=None):
    for q in chunks(a) if which is None else which:
        mid, res = residual_at(a, aux, src, q)
        for k in range(3):
            dst[k, 8 + 8 * q : 16 + 8 * q] = mid[k] + aux[3 + k, 8 * q : 8 * q + 8] * res[k]


def residual(a, aux, v, r):
    height = a.shape[1]
    for q in chunks(a):
        _, res = residual_at(a, aux, v, q)
        for k in range(3):
            r[k * height + 8 * q : k * height + 8 * q + 8, :] = res[k]


def pool_lanes(x, matrix, tail=None):
    n = matrix.shape[0]
    width = x.shape[1]
    parts = []
    for b in range(0, width, n):
        if b + n <= width:
            parts.append(dot(x[:, b : b + n], matrix))
        else:
            parts.append(dot(x[:, b:width], matrix[: width - b] if tail is None else tail))
    return parts


def pool_rows(parts, st, odd=False):
    st = st()
    out = []
    for b, part in enumerate(parts):
        n = part.shape[0]
        st[b, 0:n, :] = part
        top = st[b, pl.ds(1, n // 2, stride=2), :]
        out.append(top if odd else top + st[b, pl.ds(0, n // 2, stride=2), :])
    return out


def coarsen_coefficients(arrays, st, even, odd):
    h = arrays[0].shape[0]
    parts = pool_lanes(jnp.concatenate(arrays[:7], 0), even)
    noise = pool_rows([p[: 6 * h] for p in parts], st)
    down = pool_rows([p[6 * h :] for p in parts], st, odd=True)
    right = pool_rows(pool_lanes(arrays[7], odd), st)
    h = h // 2
    out = []
    for i in range(6):
        out.append([p[i * h : i * h + h] for p in noise])
    return out + [down, right]


def spread_rows(parts, st):
    st = st()
    for b, part in enumerate(parts):
        n = part.shape[0]
        st[b, pl.ds(0, n, stride=2), :] = part
        st[b, pl.ds(1, n, stride=2), :] = part
    return st


def put(a, channel, row, parts, tile=0):
    for b, part in enumerate(parts, tile):
        a[channel, row : row + part.shape[0], SIDE * b : SIDE * b + SIDE] = part


def add_spread(v, dst, st, stride, blocks, height, row0=0):
    for k in range(3):
        for b in range(blocks):
            lanes = slice(SIDE * b, SIDE * b + SIDE)
            dst[k, 8 : 8 + height, lanes] = v[k, 8 : 8 + height, lanes] + st[b, stride * k + row0 : stride * k + row0 + height, :]


def kernel(
    T, NB, NS, stack, out,
    a0, x0, u0, w0, r0, a1, x1, u1, w1, r1, a2, x2, u2, w2, r2, a3, x3, u3, w3, r3, a4, x4, u4, w4,
    tiles, win, sent, got, rows_sent, rows_got,
    coef_own, coef_side, coef_pack, src_own, src_side, src_pack, side_rows,
    in_sem, halo_send, halo_recv, coef_send, coef_recv, src_send, src_recv, row_send, row_recv,
):
    turn = itertools.cycle(range(BUFFERS))

    def st():
        return tiles.at[next(turn)]

    t = lax.axis_index("tiles")
    col = lax.axis_index("band") * NS + lax.axis_index("stokes")
    cols = NB * NS
    h, w = stack.shape[1], stack.shape[2]
    has = {-1: col > 0, 0: None, 1: col < cols - 1}
    rowhas = {-1: t > 0, 0: None, 1: t < T - 1}

    def when(*conds):
        conds = [c for c in conds if c is not None]
        if not conds:
            return lambda f: f()
        return pl.when(functools.reduce(jnp.logical_and, conds))

    def device(tile, dc):
        c = col + dc
        return {"tiles": tile, "band": c // NS, "stokes": lax.rem(c, NS)}

    own_rows, own_cols = slice(HALO, HALO + h), slice(0, w)
    load = pltpu.make_async_copy(stack, a0.at[:, own_rows, own_cols], in_sem.at[0])
    load.start()

    partners = [(dt, dc) for dc in (0, -1, 1) for dt in range(1, T)] + [(0, -1), (0, 1)]
    barrier = pltpu.get_barrier_semaphore()
    for dt, dc in partners:
        @when(has[dc])
        def _(dt=dt, dc=dc):
            pl.semaphore_signal(barrier, inc=1, device_id=device(lax.rem(t + dt, T), dc), device_id_type=MESH)


    lane = iota((8, SIDE), 1)
    for q in range(h // 8):
        rows = slice(8 * q, 8 * q + 8)
        head = tail = jnp.zeros((8, SIDE), F32)
        for i in range(11):
            here = (lane >= DEEP * i) & (lane < DEEP * i + DEEP)
            one, two = stack[i, rows, 0:SIDE], stack[i, rows, w - SIDE : w]
            head = jnp.where(here, pltpu.roll(one, DEEP * i, 1) if i else one, head)
            tail = jnp.where(here, pltpu.roll(two, (DEEP * i + DEEP) % SIDE, 1), tail)
        sent[0, 8 * q : 8 * q + 8], sent[1, 8 * q : 8 * q + 8] = head, tail
    at = 0
    for i, n in enumerate(NEAR_ROWS):
        rows_sent[0, at : at + n] = stack[i, 0:n]
        rows_sent[1, at : at + n] = stack[i, h - n : h]
        at += n

    sides = 1 + jnp.where(col > 0, 1, 0) + jnp.where(col < cols - 1, 1, 0)
    pl.semaphore_wait(barrier, sides * T - 1)

    row_dst = {-1: slice(HALO + h, 2 * HALO + h), 0: own_rows, 1: slice(0, HALO)}
    part_src = {-1: slice(0, HALO), 0: slice(0, h), 1: slice(h - HALO, h)}

    def halo(dr, dc):
        i = (dr + 1) * 3 + dc + 1
        if dc:
            src = sent.at[(dc + 1) // 2, part_src[dr]]
            dst = got.at[(1 - dc) // 2, row_dst[dr]]
        else:
            src, dst = rows_sent.at[(dr + 1) // 2], rows_got.at[(1 - dr) // 2]
        return pltpu.make_async_remote_copy(
            src_ref=src,
            dst_ref=dst,
            send_sem=halo_send.at[i],
            recv_sem=halo_recv.at[i],
            device_id=device(t + dr, dc),
            device_id_type=MESH,
        )

    ways = [(0, -1), (0, 1), (-1, -1), (-1, 1), (1, -1), (1, 1), (-1, 0), (1, 0)]
    for dr, dc in ways:
        @when(rowhas[dr], has[dc])
        def _(dr=dr, dc=dc):
            halo(dr, dc).start()

    @pl.when(t == 0)
    def _():
        got[:, 0:HALO] = jnp.zeros_like(got[:, 0:HALO])
        side_rows[0] = jnp.zeros_like(side_rows[0])

    @pl.when(t == T - 1)
    def _():
        got[:, HALO + h :] = jnp.zeros_like(got[:, HALO + h :])
        side_rows[1] = jnp.zeros_like(side_rows[1])

    @pl.when(col == 0)
    def _():
        got[0] = jnp.zeros_like(got[0])
        coef_side[:, 0] = jnp.zeros_like(coef_side[:, 0])
        src_side[:, 0] = jnp.zeros_like(src_side[:, 0])

    @pl.when(col == cols - 1)
    def _():
        got[1] = jnp.zeros_like(got[1])
        coef_side[:, 1] = jnp.zeros_like(coef_side[:, 1])
        src_side[:, 1] = jnp.zeros_like(src_side[:, 1])

    a0[:, 0:HALO, own_cols] = jnp.zeros_like(a0[:, 0:HALO, own_cols])
    a0[:, HALO + h :, own_cols] = jnp.zeros_like(a0[:, HALO + h :, own_cols])
    for a in (a1, a3, a4):
        a[...] = jnp.zeros_like(a)
    for v in (x0, u0, x1, u1, x2, u2, x3, u3, x4, u4):
        v[:, 0:8, :] = jnp.zeros_like(v[:, 0:8, :])
        n = v.shape[1]
        v[:, n - 8 : n, :] = jnp.zeros_like(v[:, n - 8 : n, :])

    def gather(own, side, pack, send, recv, dt, dc):
        if dc:
            src, dst = pack.at[(dc + 1) // 2], side.at[t, (1 - dc) // 2]
        else:
            src, dst = own.at[t], own.at[t]
        return pltpu.make_async_remote_copy(
            src_ref=src,
            dst_ref=dst,
            send_sem=send.at[dt, dc + 1],
            recv_sem=recv.at[t, 1 - dc],
            device_id=device(lax.rem(t + dt, T), dc),
            device_id_type=MESH,
        )

    def arrival(own, side, pack, send, recv, dt, dc):
        s = lax.rem(t + dt, T)
        dst = side.at[s, (dc + 1) // 2] if dc else own.at[s]
        return pltpu.make_async_remote_copy(
            src_ref=dst,
            dst_ref=dst,
            send_sem=send.at[dt, dc + 1],
            recv_sem=recv.at[s, dc + 1],
            device_id=device(s, dc),
            device_id_type=MESH,
        )

    coef = (coef_own, coef_side, coef_pack, coef_send, coef_recv)
    src = (src_own, src_side, src_pack, src_send, src_recv)

    def scatter(x, way):
        own, pack = way[0], way[2]
        n = x.shape[0] // 2
        low = iota((n, SIDE), 1) < 64
        own[t] = x
        pack[0] = jnp.where(low, x[:n], pltpu.roll(x[n:], 64, 1))
        pack[1] = jnp.where(low, pltpu.roll(x[:n], 64, 1), x[n:])
        for dt, dc in partners:
            @when(has[dc])
            def _(dt=dt, dc=dc):
                gather(*way, dt, dc).start()

    def assemble(way, channel, count):
        for dt, dc in partners:
            @when(has[dc])
            def _(dt=dt, dc=dc):
                arrival(*way, dt, dc).wait_recv()
        own, side = way[:2]
        n = side.shape[2]
        low = iota((n, SIDE), 1) < 64

        def beside(s):
            left, right = side[s, 0], side[s, 1]
            return jnp.concatenate(
                [jnp.where(low, right, pltpu.roll(left, 64, 1)), jnp.where(low, pltpu.roll(right, 64, 1), left)], 0
            )

        for j in range(T // 2):
            for c in range(2):
                one, two = (beside(2 * j), beside(2 * j + 1)) if c else (own[2 * j], own[2 * j + 1])
                for i in range(count):
                    a2[channel + i, 8 * j : 8 * j + 8, SIDE * c : SIDE * c + SIDE] = jnp.concatenate(
                        [one[4 * i : 4 * i + 4], two[4 * i : 4 * i + 4]], 0
                    )

    even, odd = pool_matrix(256, 128), pool_matrix(256, 128, odd=True)
    even_ring, odd_ring = ring_pool(64), ring_pool(64, odd=True)
    wide = spread_matrix(128, 256)

    fine = [stack[3 + i] for i in range(8)]
    mid = coarsen_coefficients(fine, st, even, odd)
    for i in range(8):
        put(a1, 3 + i, 8, mid[i])
    mid = [jnp.concatenate(parts, 1) for parts in mid]
    low = [parts[0] for parts in coarsen_coefficients(mid, st, even, odd)]
    scatter(jnp.concatenate(low, 0), coef)

    for dr, dc in ways:
        if dc:
            @when(rowhas[dr], has[dc])
            def _(dr=dr, dc=dc):
                halo(-dr, -dc).wait_recv()

    for q in range(a0.shape[1] // 8):
        rows = slice(8 * q, 8 * q + 8)
        for i in range(11):
            right = pltpu.roll(got[1, rows], SIDE - DEEP * i, 1) if i else got[1, rows]
            left = pltpu.roll(got[0, rows], SIDE - DEEP - DEEP * i, 1)
            a0[i, rows, w : w + SIDE] = jnp.where(
                lane < DEEP, right, jnp.where(lane >= SIDE - DEEP, left, 0.0)
            )

    ends = [a0[3 + i, :, w : w + SIDE] for i in range(8)]
    for i, parts in enumerate(coarsen_coefficients(ends, st, even_ring, odd_ring)):
        put(a1, 3 + i, 4, parts, 2)

    for dr in (-1, 1):
        @when(rowhas[dr])
        def _(dr=dr):
            halo(-dr, 0).wait_recv()
            at = 0
            for i, n in enumerate(NEAR_ROWS):
                top = HALO - n if dr < 0 else HALO + h
                a0[i, top : top + n, own_cols] = rows_got[(dr + 1) // 2, at : at + n]
                at += n

    load.wait()

    setup(a0, w0)
    first(a0, w0, x0)
    sweep(a0, w0, x0, u0)
    residual(a0, w0, u0, r0)
    source = pool_rows(pool_lanes(r0[...], even, even_ring), st)
    h1 = a0.shape[1] // 2
    for k in range(3):
        put(a1, k, 4, [p[k * h1 : k * h1 + h1] for p in source])
    beside = [
        jnp.concatenate([a0[3 + i, 0:HALO, own_cols], a0[3 + i, HALO + h :, own_cols]], 0) for i in range(8)
    ]
    for i, parts in enumerate(coarsen_coefficients(beside, st, even, odd)):
        put(a1, 3 + i, 4, [p[:4] for p in parts])
        put(a1, 3 + i, 16, [p[4:] for p in parts])
    setup(a1, w1)
    first(a1, w1, x1)
    sweep(a1, w1, x1, u1)
    residual(a1, w1, u1, r1)
    own = dot(r1[:, 0:256], even)
    source = pool_rows([own], st)[0]
    packed = [source[12 * k + 4 : 12 * k + 8] for k in range(3)]
    scatter(jnp.concatenate(packed + [jnp.zeros((4, SIDE), F32)], 0), src)

    def rows_copy(dr):
        i = (dr + 1) // 2
        return pltpu.make_async_remote_copy(
            src_ref=u1.at[:, 16:24, :],
            dst_ref=side_rows.at[1 - i],
            send_sem=row_send.at[i],
            recv_sem=row_recv.at[1 - i],
            device_id=device(t + dr, 0),
            device_id_type=MESH,
        )

    for dr in (-1, 1):
        @when(rowhas[dr])
        def _(dr=dr):
            rows_copy(dr).start()

    assemble(coef, 3, 8)
    setup(a2, w2)
    last, last_odd = ring_pool(96), ring_pool(96, odd=True)
    for a, b, aux, p, p_odd in ((a2, a3, w3, even, odd), (a3, a4, w4, last, last_odd)):
        for i, parts in enumerate(coarsen_coefficients([a[3 + i] for i in range(8)], st, p, p_odd)):
            put(b, 3 + i, 0, parts)
        setup(b, aux)
    assemble(src, 0, 3)

    for a, aux, x, u, r, b, p in ((a2, w2, x2, u2, r2, a3, even), (a3, w3, x3, u3, r3, a4, last)):
        first(a, aux, x)
        sweep(a, aux, x, u)
        residual(a, aux, u, r)
        source = pool_rows(pool_lanes(r[...], p), st)
        n = a.shape[1] // 2
        for k in range(3):
            put(b, k, 0, [z[k * n : k * n + n] for z in source])
    if h // 16 * T < 8:
        n = [a4[3 + i] for i in range(6)]
        down, right, up, left, total = a4[9], a4[10], w4[0], w4[1], w4[2]
        source, scale = [a4[k] for k in range(3)], [w4[3 + k] for k in range(3)]
        v = [scale[k] * source[k] for k in range(3)]
        weight = [n[k] + total for k in range(3)]
        for _ in range(COARSE_SWEEPS - 1):
            cross = [n[3] * v[1] + n[4] * v[2], n[3] * v[0] + n[5] * v[2], n[4] * v[0] + n[5] * v[1]]
            new = []
            for k in range(3):
                near = (down * pltpu.roll(v[k], 7, 0) + up * pltpu.roll(v[k], 1, 0)) + (
                    right * pltpu.roll(v[k], SIDE - 1, 1) + left * pltpu.roll(v[k], 1, 1)
                )
                new.append(v[k] + scale[k] * (source[k] - (weight[k] * v[k] + cross[k]) + near))
            v = new
    else:
        first(a4, w4, x4)
        now, then = x4, u4
        for _ in range(COARSE_SWEEPS - 1):
            sweep(a4, w4, now, then)
            now, then = then, now
        v = [now[k, 8 : 8 + a4.shape[1]] for k in range(3)]
    for a, aux, x, u in ((a3, w3, x3, u3), (a2, w2, x2, u2)):
        n = v[0].shape[0]
        z = dot(jnp.concatenate(v, 0), wide if a is a2 else ring_spread(SIDE, SIDE, 96))
        parts = [z[:, b : b + SIDE] for b in range(0, z.shape[1], SIDE)]
        add_spread(u, x, spread_rows(parts, st), 2 * n, len(parts), a.shape[1])
        sweep(a, aux, x, u)
        sweep(a, aux, u, x)
        v = [x[k, 8 : 8 + a.shape[1]] for k in range(3)]

    for s in range(T):
        @pl.when(t == s)
        def _(s=s):
            for k in range(3):
                win[16 * k : 16 * k + 16, :] = x2[k, 4 + 4 * s : 20 + 4 * s]
    y = dot(win[...], ring_spread(256, 384, 320))
    spread = spread_rows([y[:, 128 * b : 128 * b + 128] for b in range(3)], st)
    for dr in (-1, 1):
        @when(rowhas[dr])
        def _(dr=dr):
            rows_copy(dr).wait_send()
            rows_copy(-dr).wait_recv()
    u1[:, 8:16, :] = side_rows[0]
    u1[:, 24:32, :] = side_rows[1]
    add_spread(u1, x1, spread, 32, 3, 24)
    sweep(a1, w1, x1, u1)
    sweep(a1, w1, u1, x1)

    y = jnp.concatenate([x1[k, 8:32] for k in range(3)], 0)
    parts = []
    for b in range(2):
        z = dot(y[:, 128 * b : 128 * b + 128], wide)
        parts += [z[:, :128], z[:, 128:]]
    parts.append(dot(y[:, 256:384], ring_spread(SIDE, SIDE, 64)))
    add_spread(u0, x0, spread_rows(parts, st), 48, 5, 32, row0=8)
    sweep(a0, w0, x0, u0)
    for q in range(1, 1 + h // 8):
        mid, res = residual_at(a0, w0, u0, q)
        for k in range(3):
            new = mid[k] + w0[3 + k, 8 * q : 8 * q + 8] * res[k]
            out[k, 8 * q - 8 : 8 * q, :] = new[:, own_cols]

    for dr, dc in ways:
        @when(rowhas[dr], has[dc])
        def _(dr=dr, dc=dc):
            halo(dr, dc).wait_send()
    for dt, dc in partners:
        @when(has[dc])
        def _(dt=dt, dc=dc):
            gather(*coef, dt, dc).wait_send()
            gather(*src, dt, dc).wait_send()


def on_device(right_side, noise_block, edges):
    T, NB, NS = lax.axis_size("tiles"), lax.axis_size("band"), lax.axis_size("stokes")
    _, h, w = right_side.shape
    shapes = [
        (h + 2 * HALO, w + SIDE),
        (h // 2 + 16, w // 2 + SIDE),
        (h // 4 * T, 2 * SIDE),
        (max(8, h // 8 * T), SIDE),
        (max(8, h // 16 * T), SIDE),
    ]
    scratch = []
    for i, (n, m) in enumerate(shapes):
        scratch += [
            pltpu.VMEM((11, n, m), F32),
            pltpu.VMEM((3, n + 16, m), F32),
            pltpu.VMEM((3, n + 16, m), F32),
            pltpu.VMEM((6, n, m), F32),
        ]
        if i < 4:
            scratch.append(pltpu.VMEM((3 * n, m), F32))
    scratch += [
        pltpu.VMEM((BUFFERS, 5, max(6 * 32, 6 * h // 4 * T), SIDE), F32),
        pltpu.VMEM((48, 2 * SIDE), F32),
        pltpu.VMEM((2, h, SIDE), F32),
        pltpu.VMEM((2, h + 2 * HALO, SIDE), F32),
        pltpu.VMEM((2, sum(NEAR_ROWS), w), F32),
        pltpu.VMEM((2, sum(NEAR_ROWS), w), F32),
        pltpu.VMEM((T, 32, SIDE), F32),
        pltpu.VMEM((T, 2, 16, SIDE), F32),
        pltpu.VMEM((2, 16, SIDE), F32),
        pltpu.VMEM((T, 16, SIDE), F32),
        pltpu.VMEM((T, 2, 8, SIDE), F32),
        pltpu.VMEM((2, 8, SIDE), F32),
        pltpu.VMEM((2, 3, 8, 3 * SIDE), F32),
        pltpu.SemaphoreType.DMA((1,)),
        pltpu.SemaphoreType.DMA((9,)),
        pltpu.SemaphoreType.DMA((9,)),
        pltpu.SemaphoreType.DMA((T, 3)),
        pltpu.SemaphoreType.DMA((T, 3)),
        pltpu.SemaphoreType.DMA((T, 3)),
        pltpu.SemaphoreType.DMA((T, 3)),
        pltpu.SemaphoreType.DMA((2,)),
        pltpu.SemaphoreType.DMA((2,)),
    ]
    return pl.pallas_call(
        functools.partial(kernel, T, NB, NS),
        out_shape=jax.ShapeDtypeStruct(right_side.shape, F32),
        in_specs=[pl.BlockSpec(memory_space=pltpu.VMEM)],
        out_specs=pl.BlockSpec(memory_space=pltpu.VMEM),
        scratch_shapes=scratch,
        compiler_params=pltpu.CompilerParams(
            collective_id=0, has_side_effects=True, vmem_limit_bytes=40 * 1024 * 1024
        ),
    )(jnp.concatenate([right_side, noise_block, edges], 0))


def solution(mesh):
    spec = P(None, ("groups", "tiles"), ("band", "stokes"))
    return jax.shard_map(
        on_device, mesh=mesh, in_specs=(spec, spec, spec), out_specs=spec, check_vma=False
    )
```
